128 devices in a mesh: segment: 4 (over y), hid: 32 (over z, x, core).
Axes of the slice: x: 4, y: 4, z: 4, core: 2. Of those that a mesh axis runs over, the one named last changes fastest.
Arguments:
- tokens: bfloat16 [4, 128, 8192], P(None, None, 'hid'), may hold values from -34 to 34
- cotangent: bfloat16 [4, 128, 8192], P(None, None, 'hid'), may hold values from -0.70710678 to 0.70710678
- gain: float32 [4, 8192], P('segment', 'hid'), may hold values from 0.1 to 1.9
- weight_in: bfloat16 [4, 64, 128, 512], P('segment', 'hid'), may hold values from -0.35355339 to 0.3723034
- weight_mid: bfloat16 [4, 256, 128, 128], P('segment', 'hid'), may hold values from -0.35355339 to 0.3660534
- weight_low: bfloat16 [4, 256, 128, 128], P('segment', 'hid'), may hold values from -0.35355339 to 0.3660534
- weight_out: bfloat16 [4, 64, 512, 128], P('segment', 'hid'), may hold values from -0.176776695 to 0.1814642
- order_up: int32 [4, 128], P('segment'), may hold values from 0 to 127, each once within a row
- order_down: int32 [4, 128], P('segment'), may hold values from 0 to 127, each once within a row
Outputs:
- grad_in: float32 [4, 64, 128, 512], P('segment', 'hid')
- grad_mid: float32 [4, 256, 128, 128], P('segment', 'hid')
- grad_low: float32 [4, 256, 128, 128], P('segment', 'hid')
- grad_out: float32 [4, 64, 512, 128], P('segment', 'hid')
- grad_gain: float32 [4, 8192], P('segment', 'hid')
The draws below stay inside these ranges and needn't reach their ends.
Inputs may be any that keep to these rules, and one draw needn't show every extreme that they name: `order_up`: each row holds every number of 0 to 127 once. `order_down`: each row holds every number of 0 to 127 once.
All inputs are finite; a program needn't handle non-finite values.
Results may differ from the reference program's by a relative error of at most 0.024.
Values may be sent and summed in bfloat16 or wider, within the bound.
A program may use at most 64 MiB of HBM per device.

```python
import jax
import jax.numpy as jnp
from jax import lax

D = 8192
FF = 32768
BLK = 128
TOK = 128
MB = 4
LAYERS = 4
DBLK = 64
CBLK = 256
EB = 512


def row_offsets(key_sign, key_size, low_end, high_end):
    signs = jnp.where(jax.random.bernoulli(key_sign, 0.5, (MB, TOK, 1)), 1.0, -1.0)
    return signs * jax.random.uniform(key_size, (MB, TOK, 1), jnp.float32, low_end, high_end)


def biased_weight(noise_draw, offset_level, fan_in, strength):
    return (noise_draw * fan_in ** (-0.5) + offset_level * strength / fan_in).astype(jnp.bfloat16)


def draw_tokens(key, part):
    key = jax.random.fold_in(key, 7)
    key_base, key_cols, key_rows, key_sign, key_size = jax.random.split(key, 5)
    position = jnp.arange(D, dtype=jnp.float32) / D
    columns = jnp.exp(jnp.log(3.0) * position) * jax.random.uniform(key_cols, (D,), jnp.float32, 0.6, 1.4)
    spread_rows = jnp.exp(jax.random.uniform(key_rows, (MB, TOK, 1), jnp.float32, jnp.log(0.3), jnp.log(3.0)))
    base_draw = jnp.clip(jax.random.normal(key_base, (MB, TOK, D), jnp.float32), -4.0, 4.0) + row_offsets(key_sign, key_size, 0.7, 1.3)
    return (0.5 * base_draw * columns * spread_rows).astype(jnp.bfloat16)


def draw_cotangent(key, part):
    key = jax.random.fold_in(key, 11)
    key_base, key_rows, key_sign, key_size = jax.random.split(key, 4)
    spread_rows = jnp.exp(jax.random.uniform(key_rows, (MB, TOK, 1), jnp.float32, jnp.log(0.3), jnp.log(3.0)))
    base_draw = jnp.clip(jax.random.normal(key_base, (MB, TOK, D), jnp.float32), -4.0, 4.0) + row_offsets(key_sign, key_size, 0.7, 1.3)
    return (base_draw * spread_rows * (MB * TOK) ** (-0.5)).astype(jnp.bfloat16)


def draw_weight_in(key, part):
    key = jax.random.fold_in(key, 13)
    key_noise, key_offset = jax.random.split(key)
    array_shape = (LAYERS, DBLK, BLK, EB)
    noise_draw = jnp.clip(jax.random.normal(key_noise, array_shape, jnp.float32), -4.0, 4.0)
    offset_level = jax.random.uniform(key_offset, (LAYERS, 1, 1, 1), jnp.float32, 0.7, 1.3)
    return biased_weight(noise_draw, offset_level, BLK, 1.5)


def draw_weight_mid(key, part):
    key = jax.random.fold_in(key, 17)
    key_noise, key_offset = jax.random.split(key)
    array_shape = (LAYERS, CBLK, BLK, BLK)
    noise_draw = jnp.clip(jax.random.normal(key_noise, array_shape, jnp.float32), -4.0, 4.0)
    offset_level = jax.random.uniform(key_offset, (LAYERS, 1, 1, 1), jnp.float32, 0.7, 1.3)
    return biased_weight(noise_draw, offset_level, BLK, 1.0)


def draw_weight_low(key, part):
    key = jax.random.fold_in(key, 19)
    key_noise, key_offset = jax.random.split(key)
    array_shape = (LAYERS, CBLK, BLK, BLK)
    noise_draw = jnp.clip(jax.random.normal(key_noise, array_shape, jnp.float32), -4.0, 4.0)
    offset_level = jax.random.uniform(key_offset, (LAYERS, 1, 1, 1), jnp.float32, 0.7, 1.3)
    return biased_weight(noise_draw, offset_level, BLK, 1.0)


def draw_weight_out(key, part):
    key = jax.random.fold_in(key, 23)
    key_noise, key_offset = jax.random.split(key)
    array_shape = (LAYERS, DBLK, EB, BLK)
    noise_draw = jnp.clip(jax.random.normal(key_noise, array_shape, jnp.float32), -4.0, 4.0)
    offset_level = jax.random.uniform(key_offset, (LAYERS, 1, 1, 1), jnp.float32, 0.7, 1.3)
    return biased_weight(noise_draw, offset_level, EB, 1.5)


def setup_inputs(seed: int = 0) -> dict:
    keys = jax.random.split(jax.random.key(seed), 10)
    return {
        "tokens": draw_tokens(jax.random.fold_in(keys[9], 71), 0),
        "cotangent": draw_cotangent(jax.random.fold_in(keys[9], 71), 0),
        "gain": jnp.clip(1.0 + 0.18 * jax.random.normal(keys[2], (LAYERS, D), jnp.float32), 0.1, 1.9),
        "weight_in": draw_weight_in(jax.random.fold_in(keys[9], 71), 0),
        "weight_mid": draw_weight_mid(jax.random.fold_in(keys[9], 71), 0),
        "weight_low": draw_weight_low(jax.random.fold_in(keys[9], 71), 0),
        "weight_out": draw_weight_out(jax.random.fold_in(keys[9], 71), 0),
        "order_up": jax.vmap(lambda own: jax.random.permutation(own, BLK))(jax.random.split(keys[7], LAYERS)).reshape((LAYERS, BLK)).astype(jnp.int32),
        "order_down": jax.vmap(lambda own: jax.random.permutation(own, BLK))(jax.random.split(keys[8], LAYERS)).reshape((LAYERS, BLK)).astype(jnp.int32),
    }


epsilon = 1e-05
root_two_pi = 0.7978845608028654
cubic = 0.044715

def gelu_pair(pre_act):
    inner_arg = root_two_pi * (pre_act + cubic * pre_act * pre_act * pre_act)
    tangent = jnp.tanh(inner_arg)
    gelu_value = 0.5 * pre_act * (1.0 + tangent)
    gelu_slope = 0.5 * (1.0 + tangent) + 0.5 * pre_act * (1.0 - tangent * tangent) * root_two_pi * (1.0 + 3.0 * cubic * pre_act * pre_act)
    return (gelu_value, gelu_slope)

def section_forward(rows_in, gain_row, weight_in, weight_mid, weight_low, weight_out, order_up, order_down):
    count_rows = rows_in.shape[0]
    rows_f32 = rows_in.astype(jnp.float32)
    squares = lax.optimization_barrier(jnp.sum(rows_f32 * rows_f32, axis=1, keepdims=True))
    inv_rms = lax.rsqrt(squares / D + epsilon)
    normed = (rows_f32 * inv_rms * gain_row).astype(jnp.bfloat16)
    normed_blocks = normed.reshape(count_rows, D // BLK, BLK)
    hidden = jnp.einsum('tbi,bij->tbj', normed_blocks.astype(jnp.float32), weight_in.astype(jnp.float32)).astype(jnp.bfloat16)
    columns = jnp.swapaxes(hidden.reshape(count_rows, BLK, FF // BLK), 1, 2)
    values_in = jnp.take(columns, order_up, axis=2)
    pre_act = jnp.einsum('tcq,cqk->tck', values_in.astype(jnp.float32), weight_mid.astype(jnp.float32))
    gelu_value, gelu_slope = gelu_pair(pre_act)
    activated = gelu_value.astype(jnp.bfloat16)
    lowered = jnp.einsum('tcq,cqk->tck', activated.astype(jnp.float32), weight_low.astype(jnp.float32)).astype(jnp.bfloat16)
    spread = jnp.swapaxes(jnp.take(lowered, jnp.argsort(order_down).astype(jnp.int32), axis=2), 1, 2)
    spread = spread.reshape(count_rows, D // BLK, FF * BLK // D)
    branch = jnp.einsum('tbj,bji->tbi', spread.astype(jnp.float32), weight_out.astype(jnp.float32)).reshape(count_rows, D)
    rows_out = (rows_f32 + branch).astype(jnp.bfloat16)
    return (rows_out, (rows_f32, inv_rms, normed_blocks, values_in, gelu_slope, activated, spread))

def section_backward(error_in, saved, gain_row, weight_in, weight_mid, weight_low, weight_out, order_up, order_down):
    rows_f32, inv_rms, normed_blocks, values_in, gelu_slope, activated, spread = saved
    count_rows = error_in.shape[0]
    error_blocks = error_in.reshape(count_rows, D // BLK, BLK).astype(jnp.float32)
    grad_out = jnp.einsum('tbj,tbi->bji', spread.astype(jnp.float32), error_blocks)
    d_spread = jnp.einsum('tbi,bji->tbj', error_blocks, weight_out.astype(jnp.float32)).astype(jnp.bfloat16)
    d_columns = jnp.swapaxes(d_spread.reshape(count_rows, BLK, FF // BLK), 1, 2)
    d_lowered = jnp.take(d_columns, order_down, axis=2)
    grad_low = jnp.einsum('tcq,tck->cqk', activated.astype(jnp.float32), d_lowered.astype(jnp.float32))
    d_pre = (jnp.einsum('tck,cqk->tcq', d_lowered.astype(jnp.float32), weight_low.astype(jnp.float32)) * gelu_slope).astype(jnp.bfloat16)
    grad_mid = jnp.einsum('tcq,tck->cqk', values_in.astype(jnp.float32), d_pre.astype(jnp.float32))
    d_values = jnp.einsum('tck,cqk->tcq', d_pre.astype(jnp.float32), weight_mid.astype(jnp.float32)).astype(jnp.bfloat16)
    d_hidden = jnp.swapaxes(jnp.take(d_values, jnp.argsort(order_up).astype(jnp.int32), axis=2), 1, 2)
    d_hidden = d_hidden.reshape(count_rows, D // BLK, FF * BLK // D)
    grad_in = jnp.einsum('tbi,tbj->bij', normed_blocks.astype(jnp.float32), d_hidden.astype(jnp.float32))
    d_normed = jnp.einsum('tbj,bij->tbi', d_hidden.astype(jnp.float32), weight_in.astype(jnp.float32)).reshape(count_rows, D)
    grad_gain = lax.optimization_barrier(jnp.sum(d_normed * rows_f32 * inv_rms, axis=0))
    inner_sum = lax.optimization_barrier(jnp.sum(d_normed * gain_row * rows_f32, axis=1, keepdims=True))
    error_out = (error_in.astype(jnp.float32) + inv_rms * gain_row * d_normed - rows_f32 * inv_rms ** 3 * inner_sum / D).astype(jnp.bfloat16)
    return (error_out, (grad_in, grad_mid, grad_low, grad_out, grad_gain))

def reference(tokens, cotangent, gain, weight_in, weight_mid, weight_low, weight_out, order_up, order_down):
    rows_now = tokens.reshape(MB * TOK, D)
    saved_all = []
    for section in range(LAYERS):
        rows_now, saved = section_forward(rows_now, gain[section], weight_in[section], weight_mid[section], weight_low[section], weight_out[section], order_up[section], order_down[section])
        saved_all.append(saved)
    error_now = cotangent.reshape(MB * TOK, D)
    collected = [None] * LAYERS
    for section in reversed(range(LAYERS)):
        error_now, grads_here = section_backward(error_now, saved_all[section], gain[section], weight_in[section], weight_mid[section], weight_low[section], weight_out[section], order_up[section], order_down[section])
        collected[section] = grads_here
    return (jnp.stack([entry[0] for entry in collected]), jnp.stack([entry[1] for entry in collected]), jnp.stack([entry[2] for entry in collected]), jnp.stack([entry[3] for entry in collected]), jnp.stack([entry[4] for entry in collected]))
```

```python
import functools

import jax
import jax.numpy as jnp
from jax import lax
from jax.experimental import pallas as pl
from jax.experimental.pallas import tpu as pltpu
from jax.sharding import PartitionSpec as P

MESH = pl.DeviceIdType.MESH
BF = jnp.bfloat16
F32 = jnp.float32

D = 8192
SEC = 4
PEERS = 32
LN = 128
epsilon = 1e-05
root_two_pi = 0.7978845608028654
cubic = 0.044715


def mm(left, right):
    return jnp.dot(left, right, preferred_element_type=F32)


def mm_nt(left, right):
    return lax.dot_general(left, right, (((1,), (1,)), ((), ())), preferred_element_type=F32)


def gelu_pair(u):
    inner = root_two_pi * (u + cubic * u * u * u)
    tangent = jnp.tanh(inner)
    value = 0.5 * u * (1.0 + tangent)
    slope = 0.5 * (1.0 + tangent) + 0.5 * u * (1.0 - tangent * tangent) * root_two_pi * (
        1.0 + 3.0 * cubic * u * u
    )
    return value, slope


def iota(shape, dim):
    return lax.broadcasted_iota(jnp.int32, shape, dim)


def kernel(
    tok, cot, small, win, wmid, wlow, wout,
    o_in, o_mid, o_low, o_out, o_gain,
    w_i, w_m, w_l, w_o, sm,
    t_i, t_m, t_l, t_o,
    sel_u, sel_ut, sel_d, sel_dt, g_t,
    perm, perm_t, eye,
    xs, xg, part, parts, r_s, hn,
    s_a, r_a, s_b, r_b,
    v_n, u_s, sl, a_s, g_n, zq, dz, du, e_c, sum_u,
    gs_i, gs_m, gs_l, gs_o, gs_g,
    gr_i, gr_m, gr_l, gr_o, gr_g,
    w_send, w_recv, p_send, p_recv, a_send, a_recv, b_send, b_recv, g_send, g_recv,
):
    me = lax.axis_index("hid")
    seg = lax.axis_index("segment")

    barrier = pltpu.get_barrier_semaphore()

    def greet(k, carry):
        pl.semaphore_signal(
            barrier, inc=1, device_id=(seg, lax.rem(me + k, PEERS)), device_id_type=MESH
        )
        return carry

    lax.fori_loop(1, PEERS, greet, 0)
    for k in range(1, SEC):
        pl.semaphore_signal(
            barrier, inc=1, device_id=(lax.rem(seg + k, SEC), me), device_id_type=MESH
        )
    pl.semaphore_wait(barrier, PEERS - 1 + SEC - 1)

    shared = ((small, sm), (win, w_i), (wmid, w_m), (wlow, w_l), (wout, w_o))

    def broadcast_weights():
        for n, (src, dst) in enumerate(shared):
            pltpu.make_async_copy(src, dst.at[seg], w_recv.at[seg, n]).start()
            for k in (1, 3, 2):
                pltpu.make_async_remote_copy(
                    src, dst.at[seg], w_send.at[n, k - 1], w_recv.at[seg, n],
                    device_id=(lax.rem(seg + k, SEC), me), device_id_type=MESH,
                ).start()

    def wait_weights(s):
        for n, (_, dst) in enumerate(shared):
            pltpu.make_async_copy(dst.at[s], dst.at[s], w_recv.at[s, n]).wait()

    @pl.when(seg == 0)
    def _():
        broadcast_weights()

    u256, n256 = iota((256, 256), 0), iota((256, 256), 1)
    perm[...] = jnp.where(n256 == (u256 % 4) * 64 + u256 // 4, 1.0, 0.0).astype(BF)
    perm_t[...] = jnp.where(u256 == (n256 % 4) * 64 + n256 // 4, 1.0, 0.0).astype(BF)
    eye[...] = jnp.where(iota((LN, LN), 0) == iota((LN, LN), 1), 1.0, 0.0).astype(BF)

    def prepare(s):
        g_t[s] = jnp.transpose(jnp.broadcast_to(sm[s, 0:1, :], (LN, 256)))
        for which, (sel, sel_t) in enumerate(((sel_u, sel_ut), (sel_d, sel_dt))):
            order_row = sm[s, 1:2, which * LN : (which + 1) * LN].astype(jnp.int32)
            order_flat = jnp.broadcast_to(order_row, (512, LN))
            order_col = jnp.transpose(
                jnp.broadcast_to(sm[s, 1:2, which * LN : (which + 1) * LN], (512, LN))
            ).astype(jnp.int32)
            v0 = iota((512, LN), 0)
            v1 = iota((LN, 512), 1)
            for c in range(4):
                hit_t = (order_flat == (v0 // 16) * 4 + v0 % 4) & ((v0 // 4) % 4 == c)
                sel_t[s, :, c * LN : (c + 1) * LN] = jnp.where(hit_t, 1.0, 0.0).astype(BF)
                hit = (order_col == (v1 // 16) * 4 + v1 % 4) & ((v1 // 4) % 4 == c)
                sel[s, c * LN : (c + 1) * LN, :] = jnp.where(hit, 1.0, 0.0).astype(BF)
        ident = eye[...]
        for b in range(2):
            for m in range(4):
                t_i[s, b, m * LN : (m + 1) * LN, :] = mm_nt(
                    ident, w_i[s, b, :, m * LN : (m + 1) * LN]
                ).astype(BF)
            t_o[s, b] = mm_nt(ident, w_o[s, b]).astype(BF)
        for c in range(8):
            t_m[s, c] = mm_nt(ident, w_m[s, c]).astype(BF)
            t_l[s, c] = mm_nt(ident, w_l[s, c]).astype(BF)

    def send_part(way, s):
        def one(k, carry):
            pltpu.make_async_remote_copy(
                part.at[way, s], parts.at[way, s, me], p_send.at[way, s], p_recv.at[way, s],
                device_id=(seg, lax.rem(me + k, PEERS)), device_id_type=MESH,
            ).start()
            return carry

        lax.fori_loop(1, PEERS, one, 0)
        pltpu.make_async_copy(part.at[way, s], parts.at[way, s, me], p_recv.at[way, s]).start()

    def wait_part(way, s):
        whole = parts.at[way, s]
        pltpu.make_async_copy(whole, whole, p_recv.at[way, s]).wait()
        return jnp.sum(parts[way, s].reshape(PEERS, LN), axis=0, keepdims=True)

    def send_a(way, s):
        def one(k, carry):
            to = lax.rem(me + k, PEERS)
            pltpu.make_async_remote_copy(
                s_a.at[way, s, to], r_a.at[way, s, :, me], a_send.at[way, s], a_recv.at[way, s],
                device_id=(seg, to), device_id_type=MESH,
            ).start()
            return carry

        lax.fori_loop(1, PEERS, one, 0)
        pltpu.make_async_copy(
            s_a.at[way, s, me], r_a.at[way, s, :, me], a_recv.at[way, s]
        ).start()

    def send_b(way, s):
        def one(k, carry):
            to = lax.rem(me + k, PEERS)
            pltpu.make_async_remote_copy(
                s_b.at[way, s, :, to], r_b.at[way, s, me], b_send.at[way, s], b_recv.at[way, s],
                device_id=(seg, to), device_id_type=MESH,
            ).start()
            return carry

        lax.fori_loop(1, PEERS, one, 0)
        pltpu.make_async_copy(
            s_b.at[way, s, :, me], r_b.at[way, s, me], b_recv.at[way, s]
        ).start()

    def wait_whole(ref, sem):
        pltpu.make_async_copy(ref, ref, sem).wait()

    def shuffle_out(way, s):
        for m in range(4):
            rows = jnp.concatenate([hn[l, m * 64 : (m + 1) * 64, :] for l in range(4)], axis=0)
            out = mm(perm[...], rows).astype(BF)
            s_a[way, s, m * 8 : (m + 1) * 8] = out.reshape(8, 2, 16, LN)

    def shuffle_in(way, s, store):
        for m in range(4):
            rows = r_b[way, s, m * 8 : (m + 1) * 8].reshape(256, LN)
            out = mm(perm_t[...], rows).astype(BF)
            for l in range(4):
                store(l, m, out[l * 64 : (l + 1) * 64])

    def forward(s, carry):
        wait_weights(s)

        @pl.when(seg == s + 1)
        def _():
            broadcast_weights()

        prepare(s)
        x = xs[s].astype(F32)
        part[0, s] = jnp.sum(x * x, axis=0, keepdims=True)
        send_part(0, s)
        xg[s] = (x * g_t[s]).astype(BF)
        for b in range(2):
            h = mm(t_i[s, b], xg[s, b * LN : (b + 1) * LN]).astype(BF)
            hn[2 * b] = h[:256]
            hn[2 * b + 1] = h[256:]
        shuffle_out(0, s)
        send_a(0, s)
        r = lax.rsqrt(wait_part(0, s) / D + epsilon)
        r_s[s] = r
        wait_whole(r_a.at[0, s], a_recv.at[0, s])
        for q in range(2):
            v = mm(sel_u[s], r_a[0, s, q].reshape(512, LN)).astype(BF)
            v_n[s, q * 4 : (q + 1) * 4] = v.reshape(4, LN, LN)
        for c in range(8):
            u = mm(t_m[s, c], v_n[s, c]) * r
            value, slope = gelu_pair(u)
            a = value.astype(BF)
            u_s[s, c] = u
            sl[s, c] = slope
            a_s[s, c] = a
            zq[c] = mm(t_l[s, c], a).astype(BF)
        for q in range(2):
            z = mm(sel_dt[s], zq[q * 4 : (q + 1) * 4].reshape(512, LN)).astype(BF)
            s_b[0, s, q] = z.reshape(PEERS, 16, LN)
        send_b(0, s)
        wait_whole(r_b.at[0, s], b_recv.at[0, s])

        def store(l, m, value):
            g_n[s, l, m * 64 : (m + 1) * 64, :] = value

        shuffle_in(0, s, store)

        @pl.when(s < SEC - 1)
        def _():
            for b in range(2):
                y = mm(t_o[s, b], g_n[s, 2 * b : 2 * b + 2].reshape(512, LN))
                xs[s + 1, b * LN : (b + 1) * LN] = (
                    xs[s, b * LN : (b + 1) * LN].astype(F32) + y
                ).astype(BF)

        return carry

    xs[0] = jnp.transpose(tok[seg].astype(F32)).astype(BF)
    e_c[...] = jnp.transpose(cot[seg].astype(F32))
    lax.fori_loop(0, SEC, forward, 0)

    grads = ((gs_i, gr_i), (gs_m, gr_m), (gs_l, gr_l), (gs_o, gr_o), (gs_g, gr_g))

    def ship(s, n):
        src, dst = grads[n]

        @pl.when(seg != s)
        def _():
            slot = lax.rem(seg - s + SEC - 1, SEC)
            pltpu.make_async_remote_copy(
                src.at[s], dst.at[slot], g_send.at[s, n], g_recv.at[slot, n],
                device_id=(s, me), device_id_type=MESH,
            ).start()

    def backward(i, carry):
        s = SEC - 1 - i
        own = seg == s

        def emit(out_ref, send_ref, index, value):
            @pl.when(own)
            def _():
                out_ref[index] = value

            @pl.when(jnp.logical_not(own))
            def _():
                send_ref[(s, *index)] = value.astype(BF)

        e16 = e_c[...].astype(BF)
        for b in range(2):
            dg = mm(w_o[s, b], e16[b * LN : (b + 1) * LN]).astype(BF)
            hn[2 * b] = dg[:256]
            hn[2 * b + 1] = dg[256:]
        shuffle_out(1, s)
        send_a(1, s)
        for b in range(2):
            emit(
                o_out, gs_o, (b,),
                mm_nt(g_n[s, 2 * b : 2 * b + 2].reshape(512, LN), e16[b * LN : (b + 1) * LN]),
            )
        ship(s, 3)
        r = r_s[s]
        wait_whole(r_a.at[1, s], a_recv.at[1, s])
        for q in range(2):
            d = mm(sel_d[s], r_a[1, s, q].reshape(512, LN)).astype(BF)
            dz[q * 4 : (q + 1) * 4] = d.reshape(4, LN, LN)
        sum_u[...] = jnp.zeros_like(sum_u)
        for c in range(8):
            d_pre = mm(w_l[s, c], dz[c]) * sl[s, c]
            sum_u[...] += jnp.sum(d_pre * u_s[s, c], axis=0, keepdims=True)
            du[c] = (d_pre * r).astype(BF)
            zq[c] = mm(w_m[s, c], du[c]).astype(BF)
        part[1, s] = sum_u[...]
        send_part(1, s)
        for q in range(2):
            v = mm(sel_ut[s], zq[q * 4 : (q + 1) * 4].reshape(512, LN)).astype(BF)
            s_b[1, s, q] = v.reshape(PEERS, 16, LN)
        send_b(1, s)
        for c in range(8):
            emit(o_low, gs_l, (c,), mm_nt(a_s[s, c], dz[c]))
            emit(o_mid, gs_m, (c,), mm_nt(v_n[s, c], du[c]))
        ship(s, 2)
        ship(s, 1)
        total = wait_part(1, s)
        wait_whole(r_b.at[1, s], b_recv.at[1, s])

        def store(l, m, value):
            hn[l, m * 64 : (m + 1) * 64, :] = value

        shuffle_in(1, s, store)
        scale = r * r * total / D
        for b in range(2):
            lo = b * LN
            dh = hn[2 * b : 2 * b + 2].reshape(512, LN)
            emit(o_in, gs_i, (b,), mm_nt(xg[s, lo : lo + LN], dh))
            dn = mm(w_i[s, b], dh)
            x = xs[s, lo : lo + LN].astype(F32)
            gain_grad = jnp.sum(jnp.transpose(dn * x), axis=0, keepdims=True)

            @pl.when(own)
            def _():
                o_gain[:, lo : lo + LN] = gain_grad

            @pl.when(jnp.logical_not(own))
            def _():
                gs_g[s, :, lo : lo + LN] = gain_grad

            e_c[lo : lo + LN] = (
                (e_c[lo : lo + LN] + g_t[s, lo : lo + LN] * dn - x * scale).astype(BF).astype(F32)
            )
        ship(s, 0)
        ship(s, 4)
        return carry

    lax.fori_loop(0, SEC, backward, 0)

    outs = (o_in, o_mid, o_low, o_out, o_gain)
    for n in (3, 2, 1, 0, 4):
        _, landed = grads[n]
        for slot in range(SEC - 1):
            wait_whole(landed.at[slot], g_recv.at[slot, n])
        outs[n][...] += (
            landed[0].astype(F32) + landed[1].astype(F32) + landed[2].astype(F32)
        )

    def drain(i, carry):
        way, s = i // SEC, lax.rem(i, SEC)
        wait_whole(parts.at[way, s, pl.ds(0, PEERS - 1)], p_send.at[way, s])
        wait_whole(s_a.at[way, s, pl.ds(0, PEERS - 1)], a_send.at[way, s])
        wait_whole(r_b.at[way, s, pl.ds(0, PEERS - 1)], b_send.at[way, s])
        return carry

    lax.fori_loop(0, 2 * SEC, drain, 0)
    for n, (src, _) in enumerate(shared):
        for k in range(SEC - 1):
            wait_whole(src, w_send.at[n, k])

    def drain_grads(s, carry):
        @pl.when(seg != s)
        def _():
            for n in range(5):
                wait_whole(grads[n][0].at[s], g_send.at[s, n])

        return carry

    lax.fori_loop(0, SEC, drain_grads, 0)


def shards(tokens, cotangent, gain, weight_in, weight_mid, weight_low, weight_out, up, down):
    order = jnp.concatenate([up, down], axis=1).astype(F32)
    small = jnp.concatenate([gain, order, jnp.zeros((6, 256), F32)], axis=0)
    vm = pltpu.VMEM
    dma = pltpu.SemaphoreType.DMA
    scratch = [
        vm((SEC, 2, LN, 512), BF), vm((SEC, 8, LN, LN), BF), vm((SEC, 8, LN, LN), BF),
        vm((SEC, 2, 512, LN), BF), vm((SEC, 8, 256), F32),
        vm((SEC, 2, 512, LN), BF), vm((SEC, 8, LN, LN), BF), vm((SEC, 8, LN, LN), BF),
        vm((SEC, 2, LN, 512), BF),
        vm((SEC, 512, 512), BF), vm((SEC, 512, 512), BF), vm((SEC, 512, 512), BF),
        vm((SEC, 512, 512), BF), vm((SEC, 256, LN), F32),
        vm((256, 256), BF), vm((256, 256), BF), vm((LN, LN), BF),
        vm((SEC, 256, LN), BF), vm((SEC, 256, LN), BF), vm((2, SEC, 1, LN), F32),
        vm((2, SEC, PEERS, 1, LN), F32), vm((SEC, 1, LN), F32), vm((4, 256, LN), BF),
        vm((2, SEC, PEERS, 2, 16, LN), BF), vm((2, SEC, 2, PEERS, 16, LN), BF),
        vm((2, SEC, 2, PEERS, 16, LN), BF), vm((2, SEC, PEERS, 2, 16, LN), BF),
        vm((SEC, 8, LN, LN), BF), vm((SEC, 8, LN, LN), F32), vm((SEC, 8, LN, LN), F32),
        vm((SEC, 8, LN, LN), BF), vm((SEC, 4, 256, LN), BF),
        vm((8, LN, LN), BF), vm((8, LN, LN), BF), vm((8, LN, LN), BF),
        vm((256, LN), F32), vm((1, LN), F32),
        vm((SEC, 2, LN, 512), BF), vm((SEC, 8, LN, LN), BF), vm((SEC, 8, LN, LN), BF),
        vm((SEC, 2, 512, LN), BF), vm((SEC, 1, 256), F32),
        vm((3, 2, LN, 512), BF), vm((3, 8, LN, LN), BF), vm((3, 8, LN, LN), BF),
        vm((3, 2, 512, LN), BF), vm((3, 1, 256), F32),
        dma((5, SEC - 1)), dma((SEC, 5)), dma((2, SEC)), dma((2, SEC)), dma((2, SEC)),
        dma((2, SEC)), dma((2, SEC)), dma((2, SEC)), dma((SEC, 5)), dma((3, 5)),
    ]
    whole = pl.BlockSpec(memory_space=pltpu.VMEM)
    g_in, g_mid, g_low, g_out, g_gain = pl.pallas_call(
        kernel,
        out_shape=[
            jax.ShapeDtypeStruct((2, LN, 512), F32),
            jax.ShapeDtypeStruct((8, LN, LN), F32),
            jax.ShapeDtypeStruct((8, LN, LN), F32),
            jax.ShapeDtypeStruct((2, 512, LN), F32),
            jax.ShapeDtypeStruct((1, 256), F32),
        ],
        in_specs=[whole] * 7,
        out_specs=[whole] * 5,
        scratch_shapes=scratch,
        compiler_params=pltpu.CompilerParams(
            collective_id=0, has_side_effects=True, vmem_limit_bytes=60 << 20
        ),
    )(tokens, cotangent, small, weight_in[0], weight_mid[0], weight_low[0], weight_out[0])
    return g_in[None], g_mid[None], g_low[None], g_out[None], g_gain


def solution(mesh):
    in_specs = (
        P(None, None, "hid"),
        P(None, None, "hid"),
        P("segment", "hid"),
        P("segment", "hid", None, None),
        P("segment", "hid", None, None),
        P("segment", "hid", None, None),
        P("segment", "hid", None, None),
        P("segment", None),
        P("segment", None),
    )
    out_specs = (
        P("segment", "hid", None, None),
        P("segment", "hid", None, None),
        P("segment", "hid", None, None),
        P("segment", "hid", None, None),
        P("segment", "hid"),
    )
    return jax.shard_map(shards, mesh=mesh, in_specs=in_specs, out_specs=out_specs, check_vma=False)
```

```python
import functools

import jax
import jax.numpy as jnp
from jax import lax
from jax.experimental import pallas as pl
from jax.experimental.pallas import tpu as pltpu
from jax.sharding import PartitionSpec as P

MESH = pl.DeviceIdType.MESH
BF = jnp.bfloat16
F32 = jnp.float32

D = 8192
SEC = 4
PEERS = 32
LN = 128
epsilon = 1e-05
root_two_pi = 0.7978845608028654
cubic = 0.044715


def mm(left, right):
    return jnp.dot(left, right, preferred_element_type=F32)


def mm_nt(left, right):
    return lax.dot_general(left, right, (((1,), (1,)), ((), ())), preferred_element_type=F32)


def gelu_pair(u):
    inner = root_two_pi * (u + cubic * u * u * u)
    tangent = jnp.tanh(inner)
    value = 0.5 * u * (1.0 + tangent)
    slope = 0.5 * (1.0 + tangent) + 0.5 * u * (1.0 - tangent * tangent) * root_two_pi * (
        1.0 + 3.0 * cubic * u * u
    )
    return value, slope


def iota(shape, dim):
    return lax.broadcasted_iota(jnp.int32, shape, dim)


def kernel(
    tok, cot, small, win, wmid, wlow, wout,
    o_in, o_mid, o_low, o_out, o_gain,
    w_i, w_m, w_l, w_o, sm,
    t_i, t_m, t_l, t_o,
    sel_u, sel_ut, sel_d, sel_dt, g_t,
    perm, perm_t, eye,
    xs, xg, part, parts, r_s, hn,
    s_a, r_a, s_b, r_b,
    v_n, u_s, sl, a_s, g_n, zq, dz, du, e_c, sum_u,
    gs_i, gs_m, gs_l, gs_o, gs_g,
    gh_i, gh_m, gh_l, gh_o,
    gr_i, gr_m, gr_l, gr_o, gr_g,
    w_send, w_recv, w_pass, p_send, p_recv, a_send, a_recv, b_send, b_recv,
    g_send, g_recv, h_send, h_recv, gg_send, gg_recv,
):
    me = lax.axis_index("hid")
    seg = lax.axis_index("segment")

    barrier = pltpu.get_barrier_semaphore()

    def greet(k, carry):
        pl.semaphore_signal(
            barrier, inc=1, device_id=(seg, lax.rem(me + k, PEERS)), device_id_type=MESH
        )
        return carry

    lax.fori_loop(1, PEERS, greet, 0)
    for k in range(1, SEC):
        pl.semaphore_signal(
            barrier, inc=1, device_id=(lax.rem(seg + k, SEC), me), device_id_type=MESH
        )
    pl.semaphore_wait(barrier, PEERS - 1 + SEC - 1)

    shared = ((small, sm), (win, w_i), (wmid, w_m), (wlow, w_l), (wout, w_o))

    def row_at(k):
        return (lax.rem(seg + k, SEC), me)

    def broadcast_weights():
        for n, (src, dst) in enumerate(shared):
            for k in (1, 3, 2) if n == 0 else (1, 3):
                pltpu.make_async_remote_copy(
                    src, dst.at[seg], w_send.at[n, k - 1], w_recv.at[seg, n],
                    device_id=row_at(k), device_id_type=MESH,
                ).start()
            pltpu.make_async_copy(src, dst.at[seg], w_recv.at[seg, n]).start()

    def half(ref, s, h):
        size = ref.shape[1] // 2
        return ref.at[s, pl.ds(h * size, size)]

    def take(s, n):
        dst = shared[n][1]
        wait_whole(dst.at[s], w_recv.at[s, n])
        if n == 0:
            return
        for h, k in enumerate((1, 3)):

            @pl.when(seg == lax.rem(s + k, SEC))
            def _():
                piece = half(dst, s, h)
                pltpu.make_async_remote_copy(
                    piece, piece, w_pass.at[n, h], w_recv.at[s, n],
                    device_id=row_at(k), device_id_type=MESH,
                ).start()

    @pl.when(lax.rem(seg, 2) == 0)
    def _():
        broadcast_weights()

    u256, n256 = iota((256, 256), 0), iota((256, 256), 1)
    perm[...] = jnp.where(n256 == (u256 % 4) * 64 + u256 // 4, 1.0, 0.0).astype(BF)
    perm_t[...] = jnp.where(u256 == (n256 % 4) * 64 + n256 // 4, 1.0, 0.0).astype(BF)
    eye[...] = jnp.where(iota((LN, LN), 0) == iota((LN, LN), 1), 1.0, 0.0).astype(BF)

    def prepare_in(s):
        ident = eye[...]
        for b in range(2):
            for m in range(4):
                t_i[s, b, m * LN : (m + 1) * LN, :] = mm_nt(
                    ident, w_i[s, b, :, m * LN : (m + 1) * LN]
                ).astype(BF)
        g_t[s] = jnp.transpose(jnp.broadcast_to(sm[s, 0:1, :], (LN, 256)))
        for which, (sel, sel_t) in enumerate(((sel_u, sel_ut), (sel_d, sel_dt))):
            order_row = sm[s, 1:2, which * LN : (which + 1) * LN].astype(jnp.int32)
            order_flat = jnp.broadcast_to(order_row, (512, LN))
            order_col = jnp.transpose(
                jnp.broadcast_to(sm[s, 1:2, which * LN : (which + 1) * LN], (512, LN))
            ).astype(jnp.int32)
            v0 = iota((512, LN), 0)
            v1 = iota((LN, 512), 1)
            for c in range(4):
                hit_t = (order_flat == (v0 // 16) * 4 + v0 % 4) & ((v0 // 4) % 4 == c)
                sel_t[s, :, c * LN : (c + 1) * LN] = jnp.where(hit_t, 1.0, 0.0).astype(BF)
                hit = (order_col == (v1 // 16) * 4 + v1 % 4) & ((v1 // 4) % 4 == c)
                sel[s, c * LN : (c + 1) * LN, :] = jnp.where(hit, 1.0, 0.0).astype(BF)

    def prepare_mid(s):
        ident = eye[...]
        for c in range(8):
            t_m[s, c] = mm_nt(ident, w_m[s, c]).astype(BF)
            t_l[s, c] = mm_nt(ident, w_l[s, c]).astype(BF)

    def prepare_out(s):
        ident = eye[...]
        for b in range(2):
            t_o[s, b] = mm_nt(ident, w_o[s, b]).astype(BF)

    def send_part(way, s):
        def one(k, carry):
            pltpu.make_async_remote_copy(
                part.at[way, s], parts.at[way, s, me], p_send.at[way, s], p_recv.at[way, s],
                device_id=(seg, lax.rem(me + k, PEERS)), device_id_type=MESH,
            ).start()
            return carry

        lax.fori_loop(1, PEERS, one, 0)
        pltpu.make_async_copy(part.at[way, s], parts.at[way, s, me], p_recv.at[way, s]).start()

    def wait_part(way, s):
        whole = parts.at[way, s]
        pltpu.make_async_copy(whole, whole, p_recv.at[way, s]).wait()
        return jnp.sum(parts[way, s].reshape(PEERS, LN), axis=0, keepdims=True)

    def send_a(way, s):
        def one(k, carry):
            to = lax.rem(me + k, PEERS)
            pltpu.make_async_remote_copy(
                s_a.at[way, s, to], r_a.at[way, s, :, me], a_send.at[way, s], a_recv.at[way, s],
                device_id=(seg, to), device_id_type=MESH,
            ).start()
            return carry

        lax.fori_loop(1, PEERS, one, 0)
        pltpu.make_async_copy(
            s_a.at[way, s, me], r_a.at[way, s, :, me], a_recv.at[way, s]
        ).start()

    def send_b(way, s):
        def one(k, carry):
            to = lax.rem(me + k, PEERS)
            pltpu.make_async_remote_copy(
                s_b.at[way, s, :, to], r_b.at[way, s, me], b_send.at[way, s], b_recv.at[way, s],
                device_id=(seg, to), device_id_type=MESH,
            ).start()
            return carry

        lax.fori_loop(1, PEERS, one, 0)
        pltpu.make_async_copy(
            s_b.at[way, s, :, me], r_b.at[way, s, me], b_recv.at[way, s]
        ).start()

    def wait_whole(ref, sem):
        pltpu.make_async_copy(ref, ref, sem).wait()

    def shuffle_out(way, s):
        for m in range(4):
            rows = jnp.concatenate([hn[l, m * 64 : (m + 1) * 64, :] for l in range(4)], axis=0)
            out = mm(perm[...], rows).astype(BF)
            s_a[way, s, m * 8 : (m + 1) * 8] = out.reshape(8, 2, 16, LN)

    def shuffle_in(way, s, store):
        for m in range(4):
            rows = r_b[way, s, m * 8 : (m + 1) * 8].reshape(256, LN)
            out = mm(perm_t[...], rows).astype(BF)
            for l in range(4):
                store(l, m, out[l * 64 : (l + 1) * 64])

    def start_back(s):
        e16 = e_c[...].astype(BF)
        for b in range(2):
            dg = mm(w_o[s, b], e16[b * LN : (b + 1) * LN]).astype(BF)
            hn[2 * b] = dg[:256]
            hn[2 * b + 1] = dg[256:]
        shuffle_out(1, s)
        send_a(1, s)

    def gather_g(s):
        wait_whole(r_b.at[0, s], b_recv.at[0, s])

        def store(l, m, value):
            g_n[s, l, m * 64 : (m + 1) * 64, :] = value

        shuffle_in(0, s, store)

    def forward(s, carry):
        take(s, 0)
        take(s, 1)
        prepare_in(s)
        x = xs[s].astype(F32)
        part[0, s] = jnp.sum(x * x, axis=0, keepdims=True)
        send_part(0, s)
        xg[s] = (x * g_t[s]).astype(BF)
        for b in range(2):
            h = mm(t_i[s, b], xg[s, b * LN : (b + 1) * LN]).astype(BF)
            hn[2 * b] = h[:256]
            hn[2 * b + 1] = h[256:]
        shuffle_out(0, s)
        send_a(0, s)
        take(s, 2)
        take(s, 3)

        @pl.when(seg == 2 * s + 1)
        def _():
            broadcast_weights()

        prepare_mid(s)

        @pl.when(s == SEC - 1)
        def _():
            take(s, 4)
            start_back(s)

        r = lax.rsqrt(wait_part(0, s) / D + epsilon)
        r_s[s] = r
        wait_whole(r_a.at[0, s], a_recv.at[0, s])
        for q in range(2):
            v = mm(sel_u[s], r_a[0, s, q].reshape(512, LN)).astype(BF)
            v_n[s, q * 4 : (q + 1) * 4] = v.reshape(4, LN, LN)
        for c in range(8):
            u = mm(t_m[s, c], v_n[s, c]) * r
            value, slope = gelu_pair(u)
            a = value.astype(BF)
            u_s[s, c] = u
            sl[s, c] = slope
            a_s[s, c] = a
            zq[c] = mm(t_l[s, c], a).astype(BF)
        for q in range(2):
            z = mm(sel_dt[s], zq[q * 4 : (q + 1) * 4].reshape(512, LN)).astype(BF)
            s_b[0, s, q] = z.reshape(PEERS, 16, LN)
        send_b(0, s)

        @pl.when(s < SEC - 1)
        def _():
            take(s, 4)
            prepare_out(s)
            gather_g(s)
            for b in range(2):
                y = mm(t_o[s, b], g_n[s, 2 * b : 2 * b + 2].reshape(512, LN))
                xs[s + 1, b * LN : (b + 1) * LN] = (
                    xs[s, b * LN : (b + 1) * LN].astype(F32) + y
                ).astype(BF)

        return carry

    xs[0] = jnp.transpose(tok[seg].astype(F32)).astype(BF)
    e_c[...] = jnp.transpose(cot[seg].astype(F32))
    lax.fori_loop(0, SEC, forward, 0)

    grads = (
        (gs_i, gh_i, gr_i), (gs_m, gh_m, gr_m), (gs_l, gh_l, gr_l), (gs_o, gh_o, gr_o)
    )

    def near(s, k):
        return seg == lax.rem(s + k, SEC)

    def ship_half(s, n, k, h):
        src, _, dst = grads[n]
        pltpu.make_async_remote_copy(
            half(src, s, h), half(dst, k // 2, h), g_send.at[k // 2, n, h],
            g_recv.at[k // 2, n], device_id=row_at(SEC - k), device_id_type=MESH,
        ).start()

    def ship(s, n):
        src, mid, _ = grads[n]

        @pl.when(near(s, 1))
        def _():
            ship_half(s, n, 1, 1)

        @pl.when(near(s, 3))
        def _():
            ship_half(s, n, 3, 0)

        @pl.when(near(s, 2))
        def _():
            for h, k in enumerate((3, 1)):
                pltpu.make_async_remote_copy(
                    half(src, s, h), mid.at[h], h_send.at[n, h], h_recv.at[h, n],
                    device_id=row_at(k), device_id_type=MESH,
                ).start()

    def combine(s, n):
        src, mid, _ = grads[n]
        size = src.shape[1] // 2
        for h, k in enumerate((1, 3)):

            @pl.when(near(s, k))
            def _():
                wait_whole(mid.at[h], h_recv.at[h, n])
                rows = pl.ds(h * size, size)
                src[s, rows] = (src[s, rows].astype(F32) + mid[h].astype(F32)).astype(BF)
                ship_half(s, n, k, h)

    def ship_gain(s):
        @pl.when(seg != s)
        def _():
            slot = lax.rem(seg - s + SEC - 1, SEC)
            pltpu.make_async_remote_copy(
                gs_g.at[s], gr_g.at[slot], gg_send.at[s], gg_recv.at[slot],
                device_id=(s, me), device_id_type=MESH,
            ).start()

    def backward(i, carry):
        s = SEC - 1 - i
        own = seg == s

        def emit(out_ref, send_ref, index, value):
            @pl.when(own)
            def _():
                out_ref[index] = value

            @pl.when(jnp.logical_not(own))
            def _():
                send_ref[(s, *index)] = value.astype(BF)

        e16 = e_c[...].astype(BF)

        @pl.when(i == 0)
        def _():
            gather_g(s)

        for b in range(2):
            emit(
                o_out, gs_o, (b,),
                mm_nt(g_n[s, 2 * b : 2 * b + 2].reshape(512, LN), e16[b * LN : (b + 1) * LN]),
            )
        ship(s, 3)

        @pl.when(i > 0)
        def _():
            combine(s + 1, 2)
            combine(s + 1, 1)

        r = r_s[s]
        wait_whole(r_a.at[1, s], a_recv.at[1, s])
        for q in range(2):
            d = mm(sel_d[s], r_a[1, s, q].reshape(512, LN)).astype(BF)
            dz[q * 4 : (q + 1) * 4] = d.reshape(4, LN, LN)
        sum_u[...] = jnp.zeros_like(sum_u)
        for c in range(8):
            d_pre = mm(w_l[s, c], dz[c]) * sl[s, c]
            sum_u[...] += jnp.sum(d_pre * u_s[s, c], axis=0, keepdims=True)
            du[c] = (d_pre * r).astype(BF)
            zq[c] = mm(w_m[s, c], du[c]).astype(BF)
        part[1, s] = sum_u[...]
        send_part(1, s)
        for q in range(2):
            v = mm(sel_ut[s], zq[q * 4 : (q + 1) * 4].reshape(512, LN)).astype(BF)
            s_b[1, s, q] = v.reshape(PEERS, 16, LN)
        send_b(1, s)
        for c in range(8):
            emit(o_low, gs_l, (c,), mm_nt(a_s[s, c], dz[c]))
            emit(o_mid, gs_m, (c,), mm_nt(v_n[s, c], du[c]))
        ship(s, 2)
        ship(s, 1)

        @pl.when(i > 0)
        def _():
            combine(s + 1, 0)

        combine(s, 3)
        total = wait_part(1, s)
        wait_whole(r_b.at[1, s], b_recv.at[1, s])

        def store(l, m, value):
            hn[l, m * 64 : (m + 1) * 64, :] = value

        shuffle_in(1, s, store)
        scale = r * r * total / D
        for b in range(2):
            lo = b * LN
            dh = hn[2 * b : 2 * b + 2].reshape(512, LN)
            emit(o_in, gs_i, (b,), mm_nt(xg[s, lo : lo + LN], dh))
            dn = mm(w_i[s, b], dh)
            x = xs[s, lo : lo + LN].astype(F32)
            gain_grad = jnp.sum(jnp.transpose(dn * x), axis=0, keepdims=True)

            @pl.when(own)
            def _():
                o_gain[:, lo : lo + LN] = gain_grad

            @pl.when(jnp.logical_not(own))
            def _():
                gs_g[s, :, lo : lo + LN] = gain_grad

            e_c[lo : lo + LN] = (
                (e_c[lo : lo + LN] + g_t[s, lo : lo + LN] * dn - x * scale).astype(BF).astype(F32)
            )
        ship(s, 0)
        ship_gain(s)

        @pl.when(s > 0)
        def _():
            start_back(s - 1)

        return carry

    lax.fori_loop(0, SEC, backward, 0)

    combine(0, 2)
    combine(0, 1)
    combine(0, 0)
    outs = (o_in, o_mid, o_low, o_out)
    for n in (3, 2, 1, 0):
        _, _, landed = grads[n]
        for side in range(2):
            wait_whole(landed.at[side], g_recv.at[side, n])
        outs[n][...] += landed[0].astype(F32) + landed[1].astype(F32)
    for slot in range(SEC - 1):
        wait_whole(gr_g.at[slot], gg_recv.at[slot])
    o_gain[...] += gr_g[0] + gr_g[1] + gr_g[2]

    def drain(i, carry):
        way, s = i // SEC, lax.rem(i, SEC)
        wait_whole(parts.at[way, s, pl.ds(0, PEERS - 1)], p_send.at[way, s])
        wait_whole(s_a.at[way, s, pl.ds(0, PEERS - 1)], a_send.at[way, s])
        wait_whole(r_b.at[way, s, pl.ds(0, PEERS - 1)], b_send.at[way, s])
        return carry

    lax.fori_loop(0, 2 * SEC, drain, 0)
    for n, (src, dst) in enumerate(shared):
        for k in range(SEC - 1) if n == 0 else (0, 2):
            wait_whole(src, w_send.at[n, k])
        if n > 0:
            for h in range(2):
                wait_whole(half(dst, 0, h), w_pass.at[n, h])
    for n, (_, mid, landed) in enumerate(grads):
        for h in range(2):
            wait_whole(mid.at[h], h_send.at[n, h])
            for side in range(2):
                wait_whole(half(landed, side, h), g_send.at[side, n, h])

    def drain_gain(s, carry):
        @pl.when(seg != s)
        def _():
            wait_whole(gs_g.at[s], gg_send.at[s])

        return carry

    lax.fori_loop(0, SEC, drain_gain, 0)


def shards(tokens, cotangent, gain, weight_in, weight_mid, weight_low, weight_out, up, down):
    order = jnp.concatenate([up, down], axis=1).astype(F32)
    small = jnp.concatenate([gain, order, jnp.zeros((6, 256), F32)], axis=0)
    vm = pltpu.VMEM
    dma = pltpu.SemaphoreType.DMA
    scratch = [
        vm((SEC, 2, LN, 512), BF), vm((SEC, 8, LN, LN), BF), vm((SEC, 8, LN, LN), BF),
        vm((SEC, 2, 512, LN), BF), vm((SEC, 8, 256), F32),
        vm((SEC, 2, 512, LN), BF), vm((SEC, 8, LN, LN), BF), vm((SEC, 8, LN, LN), BF),
        vm((SEC, 2, LN, 512), BF),
        vm((SEC, 512, 512), BF), vm((SEC, 512, 512), BF), vm((SEC, 512, 512), BF),
        vm((SEC, 512, 512), BF), vm((SEC, 256, LN), F32),
        vm((256, 256), BF), vm((256, 256), BF), vm((LN, LN), BF),
        vm((SEC, 256, LN), BF), vm((SEC, 256, LN), BF), vm((2, SEC, 1, LN), F32),
        vm((2, SEC, PEERS, 1, LN), F32), vm((SEC, 1, LN), F32), vm((4, 256, LN), BF),
        vm((2, SEC, PEERS, 2, 16, LN), BF), vm((2, SEC, 2, PEERS, 16, LN), BF),
        vm((2, SEC, 2, PEERS, 16, LN), BF), vm((2, SEC, PEERS, 2, 16, LN), BF),
        vm((SEC, 8, LN, LN), BF), vm((SEC, 8, LN, LN), F32), vm((SEC, 8, LN, LN), F32),
        vm((SEC, 8, LN, LN), BF), vm((SEC, 4, 256, LN), BF),
        vm((8, LN, LN), BF), vm((8, LN, LN), BF), vm((8, LN, LN), BF),
        vm((256, LN), F32), vm((1, LN), F32),
        vm((SEC, 2, LN, 512), BF), vm((SEC, 8, LN, LN), BF), vm((SEC, 8, LN, LN), BF),
        vm((SEC, 2, 512, LN), BF), vm((SEC, 1, 256), F32),
        vm((2, 1, LN, 512), BF), vm((2, 4, LN, LN), BF), vm((2, 4, LN, LN), BF),
        vm((2, 1, 512, LN), BF),
        vm((2, 2, LN, 512), BF), vm((2, 8, LN, LN), BF), vm((2, 8, LN, LN), BF),
        vm((2, 2, 512, LN), BF), vm((3, 1, 256), F32),
        dma((5, SEC - 1)), dma((SEC, 5)), dma((5, 2)),
        dma((2, SEC)), dma((2, SEC)), dma((2, SEC)),
        dma((2, SEC)), dma((2, SEC)), dma((2, SEC)),
        dma((2, 4, 2)), dma((2, 4)), dma((4, 2)), dma((2, 4)), dma((SEC,)), dma((3,)),
    ]
    whole = pl.BlockSpec(memory_space=pltpu.VMEM)
    g_in, g_mid, g_low, g_out, g_gain = pl.pallas_call(
        kernel,
        out_shape=[
            jax.ShapeDtypeStruct((2, LN, 512), F32),
            jax.ShapeDtypeStruct((8, LN, LN), F32),
            jax.ShapeDtypeStruct((8, LN, LN), F32),
            jax.ShapeDtypeStruct((2, 512, LN), F32),
            jax.ShapeDtypeStruct((1, 256), F32),
        ],
        in_specs=[whole] * 7,
        out_specs=[whole] * 5,
        scratch_shapes=scratch,
        compiler_params=pltpu.CompilerParams(
            collective_id=0, has_side_effects=True, vmem_limit_bytes=60 << 20
        ),
    )(tokens, cotangent, small, weight_in[0], weight_mid[0], weight_low[0], weight_out[0])
    return g_in[None], g_mid[None], g_low[None], g_out[None], g_gain


def solution(mesh):
    in_specs = (
        P(None, None, "hid"),
        P(None, None, "hid"),
        P("segment", "hid"),
        P("segment", "hid", None, None),
        P("segment", "hid", None, None),
        P("segment", "hid", None, None),
        P("segment", "hid", None, None),
        P("segment", None),
        P("segment", None),
    )
    out_specs = (
        P("segment", "hid", None, None),
        P("segment", "hid", None, None),
        P("segment", "hid", None, None),
        P("segment", "hid", None, None),
        P("segment", "hid"),
    )
    return jax.shard_map(shards, mesh=mesh, in_specs=in_specs, out_specs=out_specs, check_vma=False)
```

```python
import functools

import jax
import jax.numpy as jnp
from jax import lax
from jax.experimental import pallas as pl
from jax.experimental.pallas import tpu as pltpu
from jax.sharding import PartitionSpec as P

MESH = pl.DeviceIdType.MESH
BF = jnp.bfloat16
F32 = jnp.float32

D = 8192
SEC = 4
PEERS = 32
LN = 128
epsilon = 1e-05
root_two_pi = 0.7978845608028654
cubic = 0.044715


def mm(left, right):
    return jnp.dot(left, right, preferred_element_type=F32)


def mm_nt(left, right):
    return lax.dot_general(left, right, (((1,), (1,)), ((), ())), preferred_element_type=F32)


def gelu_pair(u):
    inner = root_two_pi * (u + cubic * u * u * u)
    tangent = jnp.tanh(inner)
    value = 0.5 * u * (1.0 + tangent)
    slope = 0.5 * (1.0 + tangent) + 0.5 * u * (1.0 - tangent * tangent) * root_two_pi * (
        1.0 + 3.0 * cubic * u * u
    )
    return value, slope


def iota(shape, dim):
    return lax.broadcasted_iota(jnp.int32, shape, dim)


def kernel(
    tok, cot, small, win, wmid, wlow, wout,
    o_in, o_mid, o_low, o_out, o_gain,
    w_i, w_m, w_l, w_o, sm,
    t_i, t_m, t_l, t_o,
    sel_u, sel_ut, sel_d, sel_dt, g_t,
    perm, perm_t, eye,
    xs, xg, part, parts, r_s, hn,
    s_a, r_a, s_b, r_b,
    v_n, u_s, sl, a_s, g_n, zq, dz, du, e_c, sum_u,
    gs_i, gs_m, gs_l, gs_o, gs_g,
    gh_i, gh_m, gh_l, gh_o,
    gr_i, gr_m, gr_l, gr_o, gr_g,
    w_send, w_recv, w_pass, p_send, p_recv, a_send, a_recv, b_send, b_recv,
    g_send, g_recv, h_send, h_recv, gg_send, gg_recv,
):
    me = lax.axis_index("hid")
    seg = lax.axis_index("segment")

    def peer(k):
        return lax.rem(me + 1 + k, PEERS)

    barrier = pltpu.get_barrier_semaphore()

    def greet(k, carry):
        pl.semaphore_signal(
            barrier, inc=1, device_id=(seg, lax.rem(me + k, PEERS)), device_id_type=MESH
        )
        return carry

    lax.fori_loop(1, PEERS, greet, 0)
    for k in range(1, SEC):
        pl.semaphore_signal(
            barrier, inc=1, device_id=(lax.rem(seg + k, SEC), me), device_id_type=MESH
        )
    pl.semaphore_wait(barrier, PEERS - 1 + SEC - 1)

    shared = ((small, sm), (win, w_i), (wmid, w_m), (wlow, w_l), (wout, w_o))

    def row_at(k):
        return (lax.rem(seg + k, SEC), me)

    def near(s, k):
        return seg == lax.rem(s + k, SEC)

    def half(ref, s, h):
        size = ref.shape[1] // 2
        return ref.at[s, pl.ds(h * size, size)]

    ways = (1, 3)

    def send_weights(s):
        @pl.when(seg == s)
        def _():
            for k in (1, 3, 2):
                pltpu.make_async_remote_copy(
                    small, sm.at[s], w_send.at[0, k - 1], w_recv.at[s, 0, 0],
                    device_id=row_at(k), device_id_type=MESH,
                ).start()
            pltpu.make_async_copy(small, sm.at[s], w_recv.at[s, 0, 0]).start()
            for n in range(1, 5):
                src, dst = shared[n]
                if s > 0:
                    for k in (1, 3, 2):
                        pltpu.make_async_remote_copy(
                            src, dst.at[s], w_send.at[n, k - 1], w_recv.at[s, n, 0],
                            device_id=row_at(k), device_id_type=MESH,
                        ).start()
                    pltpu.make_async_copy(src, dst.at[s], w_recv.at[s, n, 0]).start()
                    continue
                size = src.shape[0] // 2
                for h in range(2):
                    pltpu.make_async_remote_copy(
                        src.at[pl.ds(h * size, size)], half(dst, s, h), w_send.at[n, h],
                        w_recv.at[s, n, h], device_id=row_at(ways[h]), device_id_type=MESH,
                    ).start()
                for h in range(2):
                    pltpu.make_async_copy(
                        src.at[pl.ds(h * size, size)], half(dst, s, h), w_recv.at[s, n, h]
                    ).start()

    def arrived(s, n, h):
        wait_whole(half(shared[n][1], s, h), w_recv.at[s, n, h])

    def pass_on(s, n, h, slot):
        piece = half(shared[n][1], s, h)
        pltpu.make_async_remote_copy(
            piece, piece, w_pass.at[n, slot], w_recv.at[s, n, h],
            device_id=row_at(ways[h]), device_id_type=MESH,
        ).start()

    def second(s, n):
        for h in range(2):

            @pl.when(near(s, ways[h]))
            def _():
                arrived(s, n, h)
                pass_on(s, n, h, h)

    def third(s, n):
        @pl.when(near(s, 2))
        def _():
            for h in range(2):
                arrived(s, n, h)
                pass_on(s, n, h, 2 + h)

    def final(s, n):
        if s > 0:
            wait_whole(shared[n][1].at[s], w_recv.at[s, n, 0])
            return

        @pl.when(near(s, 0))
        def _():
            arrived(s, n, 0)
            arrived(s, n, 1)

        for h in range(2):

            @pl.when(near(s, ways[1 - h]))
            def _():
                arrived(s, n, h)

    def final_small(s):
        wait_whole(sm.at[s], w_recv.at[s, 0, 0])

    send_weights(0)

    u256, n256 = iota((256, 256), 0), iota((256, 256), 1)
    perm[...] = jnp.where(n256 == (u256 % 4) * 64 + u256 // 4, 1.0, 0.0).astype(BF)
    perm_t[...] = jnp.where(u256 == (n256 % 4) * 64 + n256 // 4, 1.0, 0.0).astype(BF)
    eye[...] = jnp.where(iota((LN, LN), 0) == iota((LN, LN), 1), 1.0, 0.0).astype(BF)

    def prepare_in(s):
        ident = eye[...]
        for b in range(2):
            for m in range(4):
                t_i[s, b, m * LN : (m + 1) * LN, :] = mm_nt(
                    ident, w_i[s, b, :, m * LN : (m + 1) * LN]
                ).astype(BF)
        g_t[s] = jnp.transpose(jnp.broadcast_to(sm[s, 0:1, :], (LN, 256)))
        for which, (sel, sel_t) in enumerate(((sel_u, sel_ut), (sel_d, sel_dt))):
            order_row = sm[s, 1:2, which * LN : (which + 1) * LN].astype(jnp.int32)
            order_flat = jnp.broadcast_to(order_row, (512, LN))
            order_col = jnp.transpose(
                jnp.broadcast_to(sm[s, 1:2, which * LN : (which + 1) * LN], (512, LN))
            ).astype(jnp.int32)
            v0 = iota((512, LN), 0)
            v1 = iota((LN, 512), 1)
            for c in range(4):
                hit_t = (order_flat == (v0 // 16) * 4 + v0 % 4) & ((v0 // 4) % 4 == c)
                sel_t[s, :, c * LN : (c + 1) * LN] = jnp.where(hit_t, 1.0, 0.0).astype(BF)
                hit = (order_col == (v1 // 16) * 4 + v1 % 4) & ((v1 // 4) % 4 == c)
                sel[s, c * LN : (c + 1) * LN, :] = jnp.where(hit, 1.0, 0.0).astype(BF)

    def prepare_mid(s):
        ident = eye[...]
        for c in range(8):
            t_m[s, c] = mm_nt(ident, w_m[s, c]).astype(BF)
            t_l[s, c] = mm_nt(ident, w_l[s, c]).astype(BF)

    def prepare_out(s):
        ident = eye[...]
        for b in range(2):
            t_o[s, b] = mm_nt(ident, w_o[s, b]).astype(BF)

    def send_part(way, s):
        def one(k, carry):
            pltpu.make_async_remote_copy(
                part.at[way, s], parts.at[way, s, me], p_send.at[way, s], p_recv.at[way, s],
                device_id=(seg, peer(k)), device_id_type=MESH,
            ).start()
            return carry

        lax.fori_loop(0, PEERS - 1, one, 0)
        pltpu.make_async_copy(part.at[way, s], parts.at[way, s, me], p_recv.at[way, s]).start()

    def wait_part(way, s):
        whole = parts.at[way, s]
        pltpu.make_async_copy(whole, whole, p_recv.at[way, s]).wait()
        return jnp.sum(parts[way, s].reshape(PEERS, LN), axis=0, keepdims=True)

    def send_a(way, s):
        for q in range(2):

            def one(k, carry):
                to = peer(k)
                pltpu.make_async_remote_copy(
                    s_a.at[way, s, to, q], r_a.at[way, s, q, me], a_send.at[way, s],
                    a_recv.at[way, s, q], device_id=(seg, to), device_id_type=MESH,
                ).start()
                return carry

            lax.fori_loop(0, PEERS - 1, one, 0)
            pltpu.make_async_copy(
                s_a.at[way, s, me, q], r_a.at[way, s, q, me], a_recv.at[way, s, q]
            ).start()

    def send_b(way, s, q):
        def one(k, carry):
            to = peer(k)
            pltpu.make_async_remote_copy(
                s_b.at[way, s, q, to], r_b.at[way, s, me, q], b_send.at[way, s],
                b_recv.at[way, s], device_id=(seg, to), device_id_type=MESH,
            ).start()
            return carry

        lax.fori_loop(0, PEERS - 1, one, 0)
        pltpu.make_async_copy(
            s_b.at[way, s, q, me], r_b.at[way, s, me, q], b_recv.at[way, s]
        ).start()

    def wait_whole(ref, sem):
        pltpu.make_async_copy(ref, ref, sem).wait()

    def shuffle_out(way, s):
        for m in range(4):
            rows = jnp.concatenate([hn[l, m * 64 : (m + 1) * 64, :] for l in range(4)], axis=0)
            out = mm(perm[...], rows).astype(BF)
            s_a[way, s, m * 8 : (m + 1) * 8] = out.reshape(8, 2, 16, LN)

    def shuffle_in(way, s, store):
        for m in range(4):
            rows = r_b[way, s, m * 8 : (m + 1) * 8].reshape(256, LN)
            out = mm(perm_t[...], rows).astype(BF)
            for l in range(4):
                store(l, m, out[l * 64 : (l + 1) * 64])

    def start_back(s):
        e16 = e_c[...].astype(BF)
        for b in range(2):
            dg = mm(w_o[s, b], e16[b * LN : (b + 1) * LN]).astype(BF)
            hn[2 * b] = dg[:256]
            hn[2 * b + 1] = dg[256:]
        shuffle_out(1, s)
        send_a(1, s)

    def gather_g(s):
        wait_whole(r_b.at[0, s], b_recv.at[0, s])

        def store(l, m, value):
            g_n[s, l, m * 64 : (m + 1) * 64, :] = value

        shuffle_in(0, s, store)

    def after_a(s):
        if s == 0:
            second(0, 2)
            third(0, 2)
            for n in (3, 4):
                second(0, n)
                third(0, n)
            send_weights(1)
            send_weights(2)
        final(s, 2)
        final(s, 3)
        prepare_mid(s)

    def after_b(s):
        if s == 0:
            send_weights(3)
        final(s, 4)
        prepare_out(s)
        final_small(s + 1)
        final(s + 1, 1)
        prepare_in(s + 1)

    def forward(s):
        x = xs[s].astype(F32)
        part[0, s] = jnp.sum(x * x, axis=0, keepdims=True)
        send_part(0, s)
        xg[s] = (x * g_t[s]).astype(BF)
        for b in range(2):
            h = mm(t_i[s, b], xg[s, b * LN : (b + 1) * LN]).astype(BF)
            hn[2 * b] = h[:256]
            hn[2 * b + 1] = h[256:]
        shuffle_out(0, s)
        send_a(0, s)
        after_a(s)
        if s == SEC - 1:
            final(s, 4)
            start_back(s)
        r = lax.rsqrt(wait_part(0, s) / D + epsilon)
        r_s[s] = r
        for q in range(2):
            wait_whole(r_a.at[0, s, q], a_recv.at[0, s, q])
            v = mm(sel_u[s], r_a[0, s, q].reshape(512, LN)).astype(BF)
            v_n[s, q * 4 : (q + 1) * 4] = v.reshape(4, LN, LN)
            for c in range(q * 4, q * 4 + 4):
                u = mm(t_m[s, c], v_n[s, c]) * r
                value, slope = gelu_pair(u)
                a = value.astype(BF)
                u_s[s, c] = u
                sl[s, c] = slope
                a_s[s, c] = a
                zq[c] = mm(t_l[s, c], a).astype(BF)
            z = mm(sel_dt[s], zq[q * 4 : (q + 1) * 4].reshape(512, LN)).astype(BF)
            s_b[0, s, q] = z.reshape(PEERS, 16, LN)
            send_b(0, s, q)
        if s < SEC - 1:
            after_b(s)
            gather_g(s)
            for b in range(2):
                y = mm(t_o[s, b], g_n[s, 2 * b : 2 * b + 2].reshape(512, LN))
                xs[s + 1, b * LN : (b + 1) * LN] = (
                    xs[s, b * LN : (b + 1) * LN].astype(F32) + y
                ).astype(BF)

    xs[0] = jnp.transpose(tok[seg].astype(F32)).astype(BF)
    e_c[...] = jnp.transpose(cot[seg].astype(F32))
    second(0, 1)
    third(0, 1)
    final_small(0)
    final(0, 1)
    prepare_in(0)
    for s in range(SEC):
        forward(s)

    grads = (
        (gs_i, gh_i, gr_i), (gs_m, gh_m, gr_m), (gs_l, gh_l, gr_l), (gs_o, gh_o, gr_o)
    )

    def ship_half(s, n, k, h):
        src, _, dst = grads[n]
        pltpu.make_async_remote_copy(
            half(src, s, h), half(dst, k // 2, h), g_send.at[k // 2, n, h],
            g_recv.at[k // 2, n], device_id=row_at(SEC - k), device_id_type=MESH,
        ).start()

    def ship(s, n):
        src, mid, _ = grads[n]

        @pl.when(near(s, 1))
        def _():
            ship_half(s, n, 1, 1)

        @pl.when(near(s, 3))
        def _():
            ship_half(s, n, 3, 0)

        @pl.when(near(s, 2))
        def _():
            for h, k in enumerate((3, 1)):
                pltpu.make_async_remote_copy(
                    half(src, s, h), mid.at[h], h_send.at[n, h], h_recv.at[h, n],
                    device_id=row_at(k), device_id_type=MESH,
                ).start()

    def combine(s, n):
        src, mid, _ = grads[n]
        size = src.shape[1] // 2
        for h, k in enumerate((1, 3)):

            @pl.when(near(s, k))
            def _():
                wait_whole(mid.at[h], h_recv.at[h, n])
                rows = pl.ds(h * size, size)
                src[s, rows] = (src[s, rows].astype(F32) + mid[h].astype(F32)).astype(BF)
                ship_half(s, n, k, h)

    def ship_gain(s):
        @pl.when(seg != s)
        def _():
            slot = lax.rem(seg - s + SEC - 1, SEC)
            pltpu.make_async_remote_copy(
                gs_g.at[s], gr_g.at[slot], gg_send.at[s], gg_recv.at[slot],
                device_id=(s, me), device_id_type=MESH,
            ).start()

    def backward(i, carry):
        s = SEC - 1 - i
        own = seg == s

        def emit(out_ref, send_ref, index, value):
            @pl.when(own)
            def _():
                out_ref[index] = value

            @pl.when(jnp.logical_not(own))
            def _():
                send_ref[(s, *index)] = value.astype(BF)

        e16 = e_c[...].astype(BF)

        @pl.when(i == 0)
        def _():
            gather_g(s)

        for b in range(2):
            emit(
                o_out, gs_o, (b,),
                mm_nt(g_n[s, 2 * b : 2 * b + 2].reshape(512, LN), e16[b * LN : (b + 1) * LN]),
            )
        ship(s, 3)

        @pl.when(i > 0)
        def _():
            combine(s + 1, 2)
            combine(s + 1, 1)

        r = r_s[s]
        sum_u[...] = jnp.zeros_like(sum_u)
        for q in range(2):
            wait_whole(r_a.at[1, s, q], a_recv.at[1, s, q])
            d = mm(sel_d[s], r_a[1, s, q].reshape(512, LN)).astype(BF)
            dz[q * 4 : (q + 1) * 4] = d.reshape(4, LN, LN)
            for c in range(q * 4, q * 4 + 4):
                d_pre = mm(w_l[s, c], dz[c]) * sl[s, c]
                sum_u[...] += jnp.sum(d_pre * u_s[s, c], axis=0, keepdims=True)
                du[c] = (d_pre * r).astype(BF)
            if q == 1:
                part[1, s] = sum_u[...]
                send_part(1, s)
            for c in range(q * 4, q * 4 + 4):
                zq[c] = mm(w_m[s, c], du[c]).astype(BF)
            v = mm(sel_ut[s], zq[q * 4 : (q + 1) * 4].reshape(512, LN)).astype(BF)
            s_b[1, s, q] = v.reshape(PEERS, 16, LN)
            send_b(1, s, q)
        for c in range(8):
            emit(o_low, gs_l, (c,), mm_nt(a_s[s, c], dz[c]))
            emit(o_mid, gs_m, (c,), mm_nt(v_n[s, c], du[c]))
        ship(s, 2)
        ship(s, 1)

        @pl.when(i > 0)
        def _():
            combine(s + 1, 0)

        combine(s, 3)
        total = wait_part(1, s)
        wait_whole(r_b.at[1, s], b_recv.at[1, s])

        def store(l, m, value):
            hn[l, m * 64 : (m + 1) * 64, :] = value

        shuffle_in(1, s, store)
        scale = r * r * total / D
        for b in range(2):
            lo = b * LN
            dh = hn[2 * b : 2 * b + 2].reshape(512, LN)
            emit(o_in, gs_i, (b,), mm_nt(xg[s, lo : lo + LN], dh))
            dn = mm(w_i[s, b], dh)
            x = xs[s, lo : lo + LN].astype(F32)
            gain_grad = jnp.sum(jnp.transpose(dn * x), axis=0, keepdims=True)

            @pl.when(own)
            def _():
                o_gain[:, lo : lo + LN] = gain_grad

            @pl.when(jnp.logical_not(own))
            def _():
                gs_g[s, :, lo : lo + LN] = gain_grad

            e_c[lo : lo + LN] = (
                (e_c[lo : lo + LN] + g_t[s, lo : lo + LN] * dn - x * scale).astype(BF).astype(F32)
            )
        ship(s, 0)
        ship_gain(s)

        @pl.when(s > 0)
        def _():
            start_back(s - 1)

        return carry

    lax.fori_loop(0, SEC, backward, 0)

    combine(0, 2)
    combine(0, 1)
    combine(0, 0)
    outs = (o_in, o_mid, o_low, o_out)
    for n in (3, 2, 1, 0):
        _, _, landed = grads[n]
        for side in range(2):
            wait_whole(landed.at[side], g_recv.at[side, n])
        outs[n][...] += landed[0].astype(F32) + landed[1].astype(F32)
    for slot in range(SEC - 1):
        wait_whole(gr_g.at[slot], gg_recv.at[slot])
    o_gain[...] += gr_g[0] + gr_g[1] + gr_g[2]

    def drain(i, carry):
        way, s = i // SEC, lax.rem(i, SEC)
        wait_whole(parts.at[way, s, pl.ds(0, PEERS - 1)], p_send.at[way, s])
        wait_whole(s_a.at[way, s, pl.ds(0, PEERS - 1)], a_send.at[way, s])
        wait_whole(r_b.at[way, s, pl.ds(0, PEERS - 1)], b_send.at[way, s])
        return carry

    lax.fori_loop(0, 2 * SEC, drain, 0)
    for k in range(SEC - 1):
        wait_whole(small, w_send.at[0, k])
    def passed(*slots):
        for n in range(1, 5):
            for slot in slots:
                wait_whole(half(shared[n][1], 0, slot % 2), w_pass.at[n, slot])

    @pl.when(seg == 0)
    def _():
        for n in range(1, 5):
            for h in range(2):
                wait_whole(half(shared[n][1], 0, h), w_send.at[n, h])

    @pl.when(seg > 0)
    def _():
        for n in range(1, 5):
            for k in range(SEC - 1):
                wait_whole(shared[n][0], w_send.at[n, k])

    @pl.when(seg == 1)
    def _():
        passed(0)

    @pl.when(seg == 2)
    def _():
        passed(2, 3)

    @pl.when(seg == 3)
    def _():
        passed(1)

    for n, (_, mid, landed) in enumerate(grads):
        for h in range(2):
            wait_whole(mid.at[h], h_send.at[n, h])
            for side in range(2):
                wait_whole(half(landed, side, h), g_send.at[side, n, h])

    def drain_gain(s, carry):
        @pl.when(seg != s)
        def _():
            wait_whole(gs_g.at[s], gg_send.at[s])

        return carry

    lax.fori_loop(0, SEC, drain_gain, 0)


def shards(tokens, cotangent, gain, weight_in, weight_mid, weight_low, weight_out, up, down):
    order = jnp.concatenate([up, down], axis=1).astype(F32)
    small = jnp.concatenate([gain, order, jnp.zeros((6, 256), F32)], axis=0)
    vm = pltpu.VMEM
    dma = pltpu.SemaphoreType.DMA
    scratch = [
        vm((SEC, 2, LN, 512), BF), vm((SEC, 8, LN, LN), BF), vm((SEC, 8, LN, LN), BF),
        vm((SEC, 2, 512, LN), BF), vm((SEC, 8, 256), F32),
        vm((SEC, 2, 512, LN), BF), vm((SEC, 8, LN, LN), BF), vm((SEC, 8, LN, LN), BF),
        vm((SEC, 2, LN, 512), BF),
        vm((SEC, 512, 512), BF), vm((SEC, 512, 512), BF), vm((SEC, 512, 512), BF),
        vm((SEC, 512, 512), BF), vm((SEC, 256, LN), F32),
        vm((256, 256), BF), vm((256, 256), BF), vm((LN, LN), BF),
        vm((SEC, 256, LN), BF), vm((SEC, 256, LN), BF), vm((2, SEC, 1, LN), F32),
        vm((2, SEC, PEERS, 1, LN), F32), vm((SEC, 1, LN), F32), vm((4, 256, LN), BF),
        vm((2, SEC, PEERS, 2, 16, LN), BF), vm((2, SEC, 2, PEERS, 16, LN), BF),
        vm((2, SEC, 2, PEERS, 16, LN), BF), vm((2, SEC, PEERS, 2, 16, LN), BF),
        vm((SEC, 8, LN, LN), BF), vm((SEC, 8, LN, LN), F32), vm((SEC, 8, LN, LN), F32),
        vm((SEC, 8, LN, LN), BF), vm((SEC, 4, 256, LN), BF),
        vm((8, LN, LN), BF), vm((8, LN, LN), BF), vm((8, LN, LN), BF),
        vm((256, LN), F32), vm((1, LN), F32),
        vm((SEC, 2, LN, 512), BF), vm((SEC, 8, LN, LN), BF), vm((SEC, 8, LN, LN), BF),
        vm((SEC, 2, 512, LN), BF), vm((SEC, 1, 256), F32),
        vm((2, 1, LN, 512), BF), vm((2, 4, LN, LN), BF), vm((2, 4, LN, LN), BF),
        vm((2, 1, 512, LN), BF),
        vm((2, 2, LN, 512), BF), vm((2, 8, LN, LN), BF), vm((2, 8, LN, LN), BF),
        vm((2, 2, 512, LN), BF), vm((3, 1, 256), F32),
        dma((5, SEC - 1)), dma((SEC, 5, 2)), dma((5, 4)),
        dma((2, SEC)), dma((2, SEC)), dma((2, SEC)),
        dma((2, SEC, 2)), dma((2, SEC)), dma((2, SEC)),
        dma((2, 4, 2)), dma((2, 4)), dma((4, 2)), dma((2, 4)), dma((SEC,)), dma((3,)),
    ]
    whole = pl.BlockSpec(memory_space=pltpu.VMEM)
    g_in, g_mid, g_low, g_out, g_gain = pl.pallas_call(
        kernel,
        out_shape=[
            jax.ShapeDtypeStruct((2, LN, 512), F32),
            jax.ShapeDtypeStruct((8, LN, LN), F32),
            jax.ShapeDtypeStruct((8, LN, LN), F32),
            jax.ShapeDtypeStruct((2, 512, LN), F32),
            jax.ShapeDtypeStruct((1, 256), F32),
        ],
        in_specs=[whole] * 7,
        out_specs=[whole] * 5,
        scratch_shapes=scratch,
        compiler_params=pltpu.CompilerParams(
            collective_id=0, has_side_effects=True, vmem_limit_bytes=60 << 20
        ),
    )(tokens, cotangent, small, weight_in[0], weight_mid[0], weight_low[0], weight_out[0])
    return g_in[None], g_mid[None], g_low[None], g_out[None], g_gain


def solution(mesh):
    in_specs = (
        P(None, None, "hid"),
        P(None, None, "hid"),
        P("segment", "hid"),
        P("segment", "hid", None, None),
        P("segment", "hid", None, None),
        P("segment", "hid", None, None),
        P("segment", "hid", None, None),
        P("segment", None),
        P("segment", None),
    )
    out_specs = (
        P("segment", "hid", None, None),
        P("segment", "hid", None, None),
        P("segment", "hid", None, None),
        P("segment", "hid", None, None),
        P("segment", "hid"),
    )
    return jax.shard_map(shards, mesh=mesh, in_specs=in_specs, out_specs=out_specs, check_vma=False)
```

```python
import functools

import jax
import jax.numpy as jnp
from jax import lax
from jax.experimental import pallas as pl
from jax.experimental.pallas import tpu as pltpu
from jax.sharding import PartitionSpec as P

MESH = pl.DeviceIdType.MESH
BF = jnp.bfloat16
F32 = jnp.float32

D = 8192
SEC = 4
PEERS = 32
LN = 128
epsilon = 1e-05
root_two_pi = 0.7978845608028654
cubic = 0.044715


def mm(left, right):
    return jnp.dot(left, right, preferred_element_type=F32)


def mm_nt(left, right):
    return lax.dot_general(left, right, (((1,), (1,)), ((), ())), preferred_element_type=F32)


def gelu_pair(u):
    inner = root_two_pi * (u + cubic * u * u * u)
    tangent = jnp.tanh(inner)
    value = 0.5 * u * (1.0 + tangent)
    slope = 0.5 * (1.0 + tangent) + 0.5 * u * (1.0 - tangent * tangent) * root_two_pi * (
        1.0 + 3.0 * cubic * u * u
    )
    return value, slope


def iota(shape, dim):
    return lax.broadcasted_iota(jnp.int32, shape, dim)


def kernel(
    tok, cot, small, win, wmid, wlow, wout,
    o_in, o_mid, o_low, o_out, o_gain,
    w_i, w_m, w_l, w_o, sm,
    t_i, t_m, t_l, t_o,
    sel_u, sel_ut, sel_d, sel_dt, g_t,
    perm, perm_t, eye,
    xs, xg, part, parts, r_s, hn,
    s_a, r_a, s_b, r_b,
    v_n, u_s, sl, a_s, g_n, zq, dz, du, e_c, sum_u,
    gs_i, gs_m, gs_l, gs_o, gs_g,
    gh_i, gh_m, gh_l, gh_o,
    gr_i, gr_m, gr_l, gr_o, gr_g,
    w_send, w_recv, w_pass, p_send, p_recv, a_send, a_recv, b_send, b_recv,
    g_send, g_recv, h_send, h_recv, gg_send, gg_recv,
):
    me = lax.axis_index("hid")
    seg = lax.axis_index("segment")

    def peer(k):
        return lax.rem(me + 1 + k, PEERS)

    barrier = pltpu.get_barrier_semaphore()

    def greet(k, carry):
        pl.semaphore_signal(
            barrier, inc=1, device_id=(seg, lax.rem(me + k, PEERS)), device_id_type=MESH
        )
        return carry

    lax.fori_loop(1, PEERS, greet, 0)
    for k in range(1, SEC):
        pl.semaphore_signal(
            barrier, inc=1, device_id=(lax.rem(seg + k, SEC), me), device_id_type=MESH
        )
    pl.semaphore_wait(barrier, PEERS - 1 + SEC - 1)

    shared = ((small, sm), (win, w_i), (wmid, w_m), (wlow, w_l), (wout, w_o))

    def row_at(k):
        return (lax.rem(seg + k, SEC), me)

    def near(s, k):
        return seg == lax.rem(s + k, SEC)

    def half(ref, s, h):
        size = ref.shape[1] // 2
        return ref.at[s, pl.ds(h * size, size)]

    ways = (1, 3)

    def send_weights(s):
        @pl.when(seg == s)
        def _():
            for k in (1, 3, 2):
                pltpu.make_async_remote_copy(
                    small, sm.at[s], w_send.at[0, k - 1], w_recv.at[s, 0, 0],
                    device_id=row_at(k), device_id_type=MESH,
                ).start()
            pltpu.make_async_copy(small, sm.at[s], w_recv.at[s, 0, 0]).start()
            for n in range(1, 5):
                src, dst = shared[n]
                if s > 0:
                    for k in (1, 3, 2):
                        pltpu.make_async_remote_copy(
                            src, dst.at[s], w_send.at[n, k - 1], w_recv.at[s, n, 0],
                            device_id=row_at(k), device_id_type=MESH,
                        ).start()
                    pltpu.make_async_copy(src, dst.at[s], w_recv.at[s, n, 0]).start()
                    continue
                size = src.shape[0] // 2
                for h in range(2):
                    pltpu.make_async_remote_copy(
                        src.at[pl.ds(h * size, size)], half(dst, s, h), w_send.at[n, h],
                        w_recv.at[s, n, h], device_id=row_at(ways[h]), device_id_type=MESH,
                    ).start()
                for h in range(2):
                    pltpu.make_async_copy(
                        src.at[pl.ds(h * size, size)], half(dst, s, h), w_recv.at[s, n, h]
                    ).start()

    def arrived(s, n, h):
        wait_whole(half(shared[n][1], s, h), w_recv.at[s, n, h])

    def pass_on(s, n, h, slot):
        piece = half(shared[n][1], s, h)
        pltpu.make_async_remote_copy(
            piece, piece, w_pass.at[n, slot], w_recv.at[s, n, h],
            device_id=row_at(ways[h]), device_id_type=MESH,
        ).start()

    def second(s, n):
        for h in range(2):

            @pl.when(near(s, ways[h]))
            def _():
                arrived(s, n, h)
                pass_on(s, n, h, h)

    def third(s, n):
        @pl.when(near(s, 2))
        def _():
            for h in range(2):
                arrived(s, n, h)
                pass_on(s, n, h, 2 + h)

    def final(s, n):
        if s > 0:
            wait_whole(shared[n][1].at[s], w_recv.at[s, n, 0])
            return

        @pl.when(near(s, 0))
        def _():
            arrived(s, n, 0)
            arrived(s, n, 1)

        for h in range(2):

            @pl.when(near(s, ways[1 - h]))
            def _():
                arrived(s, n, h)

    def final_small(s):
        wait_whole(sm.at[s], w_recv.at[s, 0, 0])

    send_weights(0)

    u256, n256 = iota((256, 256), 0), iota((256, 256), 1)
    perm[...] = jnp.where(n256 == (u256 % 4) * 64 + u256 // 4, 1.0, 0.0).astype(BF)
    perm_t[...] = jnp.where(u256 == (n256 % 4) * 64 + n256 // 4, 1.0, 0.0).astype(BF)
    eye[...] = jnp.where(iota((LN, LN), 0) == iota((LN, LN), 1), 1.0, 0.0).astype(BF)

    def prepare_first(s):
        ident = eye[...]
        for b in range(2):
            for m in range(4):
                t_i[s, b, m * LN : (m + 1) * LN, :] = mm_nt(
                    ident, w_i[s, b, :, m * LN : (m + 1) * LN]
                ).astype(BF)

    def prepare_sel(s):
        g_t[s] = jnp.transpose(jnp.broadcast_to(sm[s, 0:1, :], (LN, 256)))
        for which, (sel, sel_t) in enumerate(((sel_u, sel_ut), (sel_d, sel_dt))):
            order_row = sm[s, 1:2, which * LN : (which + 1) * LN].astype(jnp.int32)
            order_flat = jnp.broadcast_to(order_row, (512, LN))
            order_col = jnp.transpose(
                jnp.broadcast_to(sm[s, 1:2, which * LN : (which + 1) * LN], (512, LN))
            ).astype(jnp.int32)
            v0 = iota((512, LN), 0)
            v1 = iota((LN, 512), 1)
            for c in range(4):
                hit_t = (order_flat == (v0 // 16) * 4 + v0 % 4) & ((v0 // 4) % 4 == c)
                sel_t[s, :, c * LN : (c + 1) * LN] = jnp.where(hit_t, 1.0, 0.0).astype(BF)
                hit = (order_col == (v1 // 16) * 4 + v1 % 4) & ((v1 // 4) % 4 == c)
                sel[s, c * LN : (c + 1) * LN, :] = jnp.where(hit, 1.0, 0.0).astype(BF)

    def prepare_mid(s):
        ident = eye[...]
        for c in range(8):
            t_m[s, c] = mm_nt(ident, w_m[s, c]).astype(BF)
            t_l[s, c] = mm_nt(ident, w_l[s, c]).astype(BF)

    def prepare_out(s):
        ident = eye[...]
        for b in range(2):
            t_o[s, b] = mm_nt(ident, w_o[s, b]).astype(BF)

    def send_part(way, s):
        def one(k, carry):
            pltpu.make_async_remote_copy(
                part.at[way, s], parts.at[way, s, me], p_send.at[way, s], p_recv.at[way, s],
                device_id=(seg, peer(k)), device_id_type=MESH,
            ).start()
            return carry

        lax.fori_loop(0, PEERS - 1, one, 0)
        pltpu.make_async_copy(part.at[way, s], parts.at[way, s, me], p_recv.at[way, s]).start()

    def wait_part(way, s):
        whole = parts.at[way, s]
        pltpu.make_async_copy(whole, whole, p_recv.at[way, s]).wait()
        return jnp.sum(parts[way, s].reshape(PEERS, LN), axis=0, keepdims=True)

    def send_a(way, s):
        for q in range(2):

            def one(k, carry):
                to = peer(k)
                pltpu.make_async_remote_copy(
                    s_a.at[way, s, to, q], r_a.at[way, s, q, me], a_send.at[way, s],
                    a_recv.at[way, s, q], device_id=(seg, to), device_id_type=MESH,
                ).start()
                return carry

            lax.fori_loop(0, PEERS - 1, one, 0)
            pltpu.make_async_copy(
                s_a.at[way, s, me, q], r_a.at[way, s, q, me], a_recv.at[way, s, q]
            ).start()

    def send_b(way, s, q):
        def one(k, carry):
            to = peer(k)
            pltpu.make_async_remote_copy(
                s_b.at[way, s, q, to], r_b.at[way, s, me, q], b_send.at[way, s],
                b_recv.at[way, s], device_id=(seg, to), device_id_type=MESH,
            ).start()
            return carry

        lax.fori_loop(0, PEERS - 1, one, 0)
        pltpu.make_async_copy(
            s_b.at[way, s, q, me], r_b.at[way, s, me, q], b_recv.at[way, s]
        ).start()

    def wait_whole(ref, sem):
        pltpu.make_async_copy(ref, ref, sem).wait()

    def shuffle_out(way, s):
        for m in range(4):
            rows = jnp.concatenate([hn[l, m * 64 : (m + 1) * 64, :] for l in range(4)], axis=0)
            out = mm(perm[...], rows).astype(BF)
            s_a[way, s, m * 8 : (m + 1) * 8] = out.reshape(8, 2, 16, LN)

    def shuffle_in(way, s, store):
        for m in range(4):
            rows = r_b[way, s, m * 8 : (m + 1) * 8].reshape(256, LN)
            out = mm(perm_t[...], rows).astype(BF)
            for l in range(4):
                store(l, m, out[l * 64 : (l + 1) * 64])

    def start_back(s):
        e16 = e_c[...].astype(BF)
        for b in range(2):
            dg = mm(w_o[s, b], e16[b * LN : (b + 1) * LN]).astype(BF)
            hn[2 * b] = dg[:256]
            hn[2 * b + 1] = dg[256:]
        shuffle_out(1, s)
        send_a(1, s)

    def gather_g(s):
        wait_whole(r_b.at[0, s], b_recv.at[0, s])

        def store(l, m, value):
            g_n[s, l, m * 64 : (m + 1) * 64, :] = value

        shuffle_in(0, s, store)

    def after_a(s):
        if s == 0:
            second(0, 2)
            third(0, 2)
            for n in (3, 4):
                second(0, n)
                third(0, n)
            send_weights(1)
            send_weights(2)
        final(s, 2)
        final(s, 3)
        prepare_mid(s)

    def after_b(s):
        if s == 0:
            send_weights(3)
        final(s, 4)
        prepare_out(s)
        final_small(s + 1)
        prepare_sel(s + 1)
        final(s + 1, 1)
        prepare_first(s + 1)

    def forward(s):
        x = xs[s].astype(F32)
        part[0, s] = jnp.sum(x * x, axis=0, keepdims=True)
        xg[s] = (x * g_t[s]).astype(BF)
        for b in range(2):
            h = mm(t_i[s, b], xg[s, b * LN : (b + 1) * LN]).astype(BF)
            hn[2 * b] = h[:256]
            hn[2 * b + 1] = h[256:]
        shuffle_out(0, s)
        send_a(0, s)
        send_part(0, s)
        after_a(s)
        if s == SEC - 1:
            final(s, 4)
            start_back(s)
        r = lax.rsqrt(wait_part(0, s) / D + epsilon)
        r_s[s] = r
        for q in range(2):
            wait_whole(r_a.at[0, s, q], a_recv.at[0, s, q])
            v = mm(sel_u[s], r_a[0, s, q].reshape(512, LN)).astype(BF)
            v_n[s, q * 4 : (q + 1) * 4] = v.reshape(4, LN, LN)
            for c in range(q * 4, q * 4 + 4):
                u = mm(t_m[s, c], v_n[s, c]) * r
                value, slope = gelu_pair(u)
                a = value.astype(BF)
                u_s[s, c] = u
                sl[s, c] = slope
                a_s[s, c] = a
                zq[c] = mm(t_l[s, c], a).astype(BF)
            z = mm(sel_dt[s], zq[q * 4 : (q + 1) * 4].reshape(512, LN)).astype(BF)
            s_b[0, s, q] = z.reshape(PEERS, 16, LN)
            send_b(0, s, q)
        if s < SEC - 1:
            after_b(s)
            gather_g(s)
            for b in range(2):
                y = mm(t_o[s, b], g_n[s, 2 * b : 2 * b + 2].reshape(512, LN))
                xs[s + 1, b * LN : (b + 1) * LN] = (
                    xs[s, b * LN : (b + 1) * LN].astype(F32) + y
                ).astype(BF)

    xs[0] = jnp.transpose(tok[seg].astype(F32)).astype(BF)
    e_c[...] = jnp.transpose(cot[seg].astype(F32))
    final_small(0)
    prepare_sel(0)
    second(0, 1)
    third(0, 1)
    final(0, 1)
    prepare_first(0)
    for s in range(SEC):
        forward(s)

    grads = (
        (gs_i, gh_i, gr_i), (gs_m, gh_m, gr_m), (gs_l, gh_l, gr_l), (gs_o, gh_o, gr_o)
    )

    def ship_half(s, n, k, h):
        src, _, dst = grads[n]
        pltpu.make_async_remote_copy(
            half(src, s, h), half(dst, k // 2, h), g_send.at[k // 2, n, h],
            g_recv.at[k // 2, n], device_id=row_at(SEC - k), device_id_type=MESH,
        ).start()

    def ship(s, n):
        src, mid, _ = grads[n]

        @pl.when(near(s, 1))
        def _():
            ship_half(s, n, 1, 1)

        @pl.when(near(s, 3))
        def _():
            ship_half(s, n, 3, 0)

        @pl.when(near(s, 2))
        def _():
            for h, k in enumerate((3, 1)):
                pltpu.make_async_remote_copy(
                    half(src, s, h), mid.at[h], h_send.at[n, h], h_recv.at[h, n],
                    device_id=row_at(k), device_id_type=MESH,
                ).start()

    def combine(s, n):
        src, mid, _ = grads[n]
        size = src.shape[1] // 2
        for h, k in enumerate((1, 3)):

            @pl.when(near(s, k))
            def _():
                wait_whole(mid.at[h], h_recv.at[h, n])
                rows = pl.ds(h * size, size)
                src[s, rows] = (src[s, rows].astype(F32) + mid[h].astype(F32)).astype(BF)
                ship_half(s, n, k, h)

    def ship_gain(s):
        @pl.when(seg != s)
        def _():
            slot = lax.rem(seg - s + SEC - 1, SEC)
            pltpu.make_async_remote_copy(
                gs_g.at[s], gr_g.at[slot], gg_send.at[s], gg_recv.at[slot],
                device_id=(s, me), device_id_type=MESH,
            ).start()

    def backward(i, carry):
        s = SEC - 1 - i
        own = seg == s

        def emit(out_ref, send_ref, index, value):
            @pl.when(own)
            def _():
                out_ref[index] = value

            @pl.when(jnp.logical_not(own))
            def _():
                send_ref[(s, *index)] = value.astype(BF)

        e16 = e_c[...].astype(BF)

        @pl.when(i == 0)
        def _():
            gather_g(s)

        for b in range(2):
            emit(
                o_out, gs_o, (b,),
                mm_nt(g_n[s, 2 * b : 2 * b + 2].reshape(512, LN), e16[b * LN : (b + 1) * LN]),
            )
        ship(s, 3)

        @pl.when(i > 0)
        def _():
            combine(s + 1, 2)
            combine(s + 1, 1)

        r = r_s[s]
        sum_u[...] = jnp.zeros_like(sum_u)
        for q in range(2):
            wait_whole(r_a.at[1, s, q], a_recv.at[1, s, q])
            d = mm(sel_d[s], r_a[1, s, q].reshape(512, LN)).astype(BF)
            dz[q * 4 : (q + 1) * 4] = d.reshape(4, LN, LN)
            for c in range(q * 4, q * 4 + 4):
                d_pre = mm(w_l[s, c], dz[c]) * sl[s, c]
                sum_u[...] += jnp.sum(d_pre * u_s[s, c], axis=0, keepdims=True)
                du[c] = (d_pre * r).astype(BF)
            for c in range(q * 4, q * 4 + 4):
                zq[c] = mm(w_m[s, c], du[c]).astype(BF)
            v = mm(sel_ut[s], zq[q * 4 : (q + 1) * 4].reshape(512, LN)).astype(BF)
            s_b[1, s, q] = v.reshape(PEERS, 16, LN)
            send_b(1, s, q)
        part[1, s] = sum_u[...]
        send_part(1, s)
        for c in range(8):
            emit(o_low, gs_l, (c,), mm_nt(a_s[s, c], dz[c]))
            emit(o_mid, gs_m, (c,), mm_nt(v_n[s, c], du[c]))
        ship(s, 2)
        ship(s, 1)

        @pl.when(i > 0)
        def _():
            combine(s + 1, 0)

        combine(s, 3)
        wait_whole(r_b.at[1, s], b_recv.at[1, s])

        def store(l, m, value):
            hn[l, m * 64 : (m + 1) * 64, :] = value

        shuffle_in(1, s, store)
        total = wait_part(1, s)
        scale = r * r * total / D
        for b in range(2):
            lo = b * LN
            dh = hn[2 * b : 2 * b + 2].reshape(512, LN)
            emit(o_in, gs_i, (b,), mm_nt(xg[s, lo : lo + LN], dh))
            dn = mm(w_i[s, b], dh)
            x = xs[s, lo : lo + LN].astype(F32)
            gain_grad = jnp.sum(jnp.transpose(dn * x), axis=0, keepdims=True)

            @pl.when(own)
            def _():
                o_gain[:, lo : lo + LN] = gain_grad

            @pl.when(jnp.logical_not(own))
            def _():
                gs_g[s, :, lo : lo + LN] = gain_grad

            e_c[lo : lo + LN] = (
                (e_c[lo : lo + LN] + g_t[s, lo : lo + LN] * dn - x * scale).astype(BF).astype(F32)
            )
        ship(s, 0)
        ship_gain(s)

        @pl.when(s > 0)
        def _():
            start_back(s - 1)

        return carry

    lax.fori_loop(0, SEC, backward, 0)

    combine(0, 2)
    combine(0, 1)
    combine(0, 0)
    outs = (o_in, o_mid, o_low, o_out)
    for n in (3, 2, 1, 0):
        _, _, landed = grads[n]
        for side in range(2):
            wait_whole(landed.at[side], g_recv.at[side, n])
        outs[n][...] += landed[0].astype(F32) + landed[1].astype(F32)
    for slot in range(SEC - 1):
        wait_whole(gr_g.at[slot], gg_recv.at[slot])
    o_gain[...] += gr_g[0] + gr_g[1] + gr_g[2]

    def drain(i, carry):
        way, s = i // SEC, lax.rem(i, SEC)
        wait_whole(parts.at[way, s, pl.ds(0, PEERS - 1)], p_send.at[way, s])
        wait_whole(s_a.at[way, s, pl.ds(0, PEERS - 1)], a_send.at[way, s])
        wait_whole(r_b.at[way, s, pl.ds(0, PEERS - 1)], b_send.at[way, s])
        return carry

    lax.fori_loop(0, 2 * SEC, drain, 0)
    for k in range(SEC - 1):
        wait_whole(small, w_send.at[0, k])
    def passed(*slots):
        for n in range(1, 5):
            for slot in slots:
                wait_whole(half(shared[n][1], 0, slot % 2), w_pass.at[n, slot])

    @pl.when(seg == 0)
    def _():
        for n in range(1, 5):
            for h in range(2):
                wait_whole(half(shared[n][1], 0, h), w_send.at[n, h])

    @pl.when(seg > 0)
    def _():
        for n in range(1, 5):
            for k in range(SEC - 1):
                wait_whole(shared[n][0], w_send.at[n, k])

    @pl.when(seg == 1)
    def _():
        passed(0)

    @pl.when(seg == 2)
    def _():
        passed(2, 3)

    @pl.when(seg == 3)
    def _():
        passed(1)

    for n, (_, mid, landed) in enumerate(grads):
        for h in range(2):
            wait_whole(mid.at[h], h_send.at[n, h])
            for side in range(2):
                wait_whole(half(landed, side, h), g_send.at[side, n, h])

    def drain_gain(s, carry):
        @pl.when(seg != s)
        def _():
            wait_whole(gs_g.at[s], gg_send.at[s])

        return carry

    lax.fori_loop(0, SEC, drain_gain, 0)


def shards(tokens, cotangent, gain, weight_in, weight_mid, weight_low, weight_out, up, down):
    order = jnp.concatenate([up, down], axis=1).astype(F32)
    small = jnp.concatenate([gain, order, jnp.zeros((6, 256), F32)], axis=0)
    vm = pltpu.VMEM
    dma = pltpu.SemaphoreType.DMA
    scratch = [
        vm((SEC, 2, LN, 512), BF), vm((SEC, 8, LN, LN), BF), vm((SEC, 8, LN, LN), BF),
        vm((SEC, 2, 512, LN), BF), vm((SEC, 8, 256), F32),
        vm((SEC, 2, 512, LN), BF), vm((SEC, 8, LN, LN), BF), vm((SEC, 8, LN, LN), BF),
        vm((SEC, 2, LN, 512), BF),
        vm((SEC, 512, 512), BF), vm((SEC, 512, 512), BF), vm((SEC, 512, 512), BF),
        vm((SEC, 512, 512), BF), vm((SEC, 256, LN), F32),
        vm((256, 256), BF), vm((256, 256), BF), vm((LN, LN), BF),
        vm((SEC, 256, LN), BF), vm((SEC, 256, LN), BF), vm((2, SEC, 1, LN), F32),
        vm((2, SEC, PEERS, 1, LN), F32), vm((SEC, 1, LN), F32), vm((4, 256, LN), BF),
        vm((2, SEC, PEERS, 2, 16, LN), BF), vm((2, SEC, 2, PEERS, 16, LN), BF),
        vm((2, SEC, 2, PEERS, 16, LN), BF), vm((2, SEC, PEERS, 2, 16, LN), BF),
        vm((SEC, 8, LN, LN), BF), vm((SEC, 8, LN, LN), F32), vm((SEC, 8, LN, LN), F32),
        vm((SEC, 8, LN, LN), BF), vm((SEC, 4, 256, LN), BF),
        vm((8, LN, LN), BF), vm((8, LN, LN), BF), vm((8, LN, LN), BF),
        vm((256, LN), F32), vm((1, LN), F32),
        vm((SEC, 2, LN, 512), BF), vm((SEC, 8, LN, LN), BF), vm((SEC, 8, LN, LN), BF),
        vm((SEC, 2, 512, LN), BF), vm((SEC, 1, 256), F32),
        vm((2, 1, LN, 512), BF), vm((2, 4, LN, LN), BF), vm((2, 4, LN, LN), BF),
        vm((2, 1, 512, LN), BF),
        vm((2, 2, LN, 512), BF), vm((2, 8, LN, LN), BF), vm((2, 8, LN, LN), BF),
        vm((2, 2, 512, LN), BF), vm((3, 1, 256), F32),
        dma((5, SEC - 1)), dma((SEC, 5, 2)), dma((5, 4)),
        dma((2, SEC)), dma((2, SEC)), dma((2, SEC)),
        dma((2, SEC, 2)), dma((2, SEC)), dma((2, SEC)),
        dma((2, 4, 2)), dma((2, 4)), dma((4, 2)), dma((2, 4)), dma((SEC,)), dma((3,)),
    ]
    whole = pl.BlockSpec(memory_space=pltpu.VMEM)
    g_in, g_mid, g_low, g_out, g_gain = pl.pallas_call(
        kernel,
        out_shape=[
            jax.ShapeDtypeStruct((2, LN, 512), F32),
            jax.ShapeDtypeStruct((8, LN, LN), F32),
            jax.ShapeDtypeStruct((8, LN, LN), F32),
            jax.ShapeDtypeStruct((2, 512, LN), F32),
            jax.ShapeDtypeStruct((1, 256), F32),
        ],
        in_specs=[whole] * 7,
        out_specs=[whole] * 5,
        scratch_shapes=scratch,
        compiler_params=pltpu.CompilerParams(
            collective_id=0, has_side_effects=True, vmem_limit_bytes=60 << 20
        ),
    )(tokens, cotangent, small, weight_in[0], weight_mid[0], weight_low[0], weight_out[0])
    return g_in[None], g_mid[None], g_low[None], g_out[None], g_gain


def solution(mesh):
    in_specs = (
        P(None, None, "hid"),
        P(None, None, "hid"),
        P("segment", "hid"),
        P("segment", "hid", None, None),
        P("segment", "hid", None, None),
        P("segment", "hid", None, None),
        P("segment", "hid", None, None),
        P("segment", None),
        P("segment", None),
    )
    out_specs = (
        P("segment", "hid", None, None),
        P("segment", "hid", None, None),
        P("segment", "hid", None, None),
        P("segment", "hid", None, None),
        P("segment", "hid"),
    )
    return jax.shard_map(shards, mesh=mesh, in_specs=in_specs, out_specs=out_specs, check_vma=False)
```

```python
import functools

import jax
import jax.numpy as jnp
from jax import lax
from jax.experimental import pallas as pl
from jax.experimental.pallas import tpu as pltpu
from jax.sharding import PartitionSpec as P

MESH = pl.DeviceIdType.MESH
BF = jnp.bfloat16
F32 = jnp.float32

D = 8192
SEC = 4
PEERS = 32
LN = 128
epsilon = 1e-05
root_two_pi = 0.7978845608028654
cubic = 0.044715


def mm(left, right):
    return jnp.dot(left, right, preferred_element_type=F32)


def mm_nt(left, right):
    return lax.dot_general(left, right, (((1,), (1,)), ((), ())), preferred_element_type=F32)


def gelu_pair(u):
    inner = root_two_pi * (u + cubic * u * u * u)
    tangent = jnp.tanh(inner)
    value = 0.5 * u * (1.0 + tangent)
    slope = 0.5 * (1.0 + tangent) + 0.5 * u * (1.0 - tangent * tangent) * root_two_pi * (
        1.0 + 3.0 * cubic * u * u
    )
    return value, slope


def iota(shape, dim):
    return lax.broadcasted_iota(jnp.int32, shape, dim)


def kernel(
    tok, cot, small, win, wmid, wlow, wout,
    o_in, o_mid, o_low, o_out, o_gain,
    w_i, w_m, w_l, w_o, sm,
    t_i, t_m, t_l, t_o,
    sel_u, sel_ut, sel_d, sel_dt, g_t,
    perm, perm_t, eye,
    xs, xg, part, parts, r_s, hn,
    s_a, r_a, s_b, r_b,
    v_n, u_s, sl, a_s, g_n, zq, dz, du, e_c, sum_u,
    gs_i, gs_m, gs_l, gs_o, gs_g,
    gh_i, gh_m, gh_l, gh_o,
    gr_i, gr_m, gr_l, gr_o, gr_g,
    w_send, w_recv, w_pass, p_send, p_recv, a_send, a_recv, b_send, b_recv,
    g_send, g_recv, h_send, h_recv, gg_send, gg_recv,
):
    me = lax.axis_index("hid")
    seg = lax.axis_index("segment")

    def peer(k):
        return lax.rem(me + 1 + k, PEERS)

    barrier = pltpu.get_barrier_semaphore()

    def greet(k, carry):
        pl.semaphore_signal(
            barrier, inc=1, device_id=(seg, lax.rem(me + k, PEERS)), device_id_type=MESH
        )
        return carry

    lax.fori_loop(1, PEERS, greet, 0)
    for k in range(1, SEC):
        pl.semaphore_signal(
            barrier, inc=1, device_id=(lax.rem(seg + k, SEC), me), device_id_type=MESH
        )
    pl.semaphore_wait(barrier, PEERS - 1 + SEC - 1)

    shared = ((small, sm), (win, w_i), (wmid, w_m), (wlow, w_l), (wout, w_o))

    def row_at(k):
        return (lax.rem(seg + k, SEC), me)

    def near(s, k):
        return seg == lax.rem(s + k, SEC)

    def half(ref, s, h):
        size = ref.shape[1] // 2
        return ref.at[s, pl.ds(h * size, size)]

    ways = (1, 3)

    def send_weights(s):
        @pl.when(seg == s)
        def _():
            for k in (1, 3, 2):
                pltpu.make_async_remote_copy(
                    small, sm.at[s], w_send.at[0, k - 1], w_recv.at[s, 0, 0],
                    device_id=row_at(k), device_id_type=MESH,
                ).start()
            pltpu.make_async_copy(small, sm.at[s], w_recv.at[s, 0, 0]).start()
            for n in range(1, 5):
                src, dst = shared[n]
                if s > 0:
                    for k in (1, 3, 2):
                        pltpu.make_async_remote_copy(
                            src, dst.at[s], w_send.at[n, k - 1], w_recv.at[s, n, 0],
                            device_id=row_at(k), device_id_type=MESH,
                        ).start()
                    pltpu.make_async_copy(src, dst.at[s], w_recv.at[s, n, 0]).start()
                    continue
                size = src.shape[0] // 2
                for h in range(2):
                    pltpu.make_async_remote_copy(
                        src.at[pl.ds(h * size, size)], half(dst, s, h), w_send.at[n, h],
                        w_recv.at[s, n, h], device_id=row_at(ways[h]), device_id_type=MESH,
                    ).start()
                for h in range(2):
                    pltpu.make_async_copy(
                        src.at[pl.ds(h * size, size)], half(dst, s, h), w_recv.at[s, n, h]
                    ).start()

    def arrived(s, n, h):
        wait_whole(half(shared[n][1], s, h), w_recv.at[s, n, h])

    def pass_on(s, n, h, slot):
        piece = half(shared[n][1], s, h)
        pltpu.make_async_remote_copy(
            piece, piece, w_pass.at[n, slot], w_recv.at[s, n, h],
            device_id=row_at(ways[h]), device_id_type=MESH,
        ).start()

    def second(s, n):
        for h in range(2):

            @pl.when(near(s, ways[h]))
            def _():
                arrived(s, n, h)
                pass_on(s, n, h, h)

    def third(s, n):
        @pl.when(near(s, 2))
        def _():
            for h in range(2):
                arrived(s, n, h)
                pass_on(s, n, h, 2 + h)

    def final(s, n):
        if s > 0:
            wait_whole(shared[n][1].at[s], w_recv.at[s, n, 0])
            return

        @pl.when(near(s, 0))
        def _():
            arrived(s, n, 0)
            arrived(s, n, 1)

        for h in range(2):

            @pl.when(near(s, ways[1 - h]))
            def _():
                arrived(s, n, h)

    def final_small(s):
        wait_whole(sm.at[s], w_recv.at[s, 0, 0])

    send_weights(0)

    u256, n256 = iota((256, 256), 0), iota((256, 256), 1)
    perm[...] = jnp.where(n256 == (u256 % 4) * 64 + u256 // 4, 1.0, 0.0).astype(BF)
    perm_t[...] = jnp.where(u256 == (n256 % 4) * 64 + n256 // 4, 1.0, 0.0).astype(BF)
    eye[...] = jnp.where(iota((LN, LN), 0) == iota((LN, LN), 1), 1.0, 0.0).astype(BF)

    def prepare_in(s):
        ident = eye[...]
        for b in range(2):
            for m in range(4):
                t_i[s, b, m * LN : (m + 1) * LN, :] = mm_nt(
                    ident, w_i[s, b, :, m * LN : (m + 1) * LN]
                ).astype(BF)
        g_t[s] = jnp.transpose(jnp.broadcast_to(sm[s, 0:1, :], (LN, 256)))
        for which, (sel, sel_t) in enumerate(((sel_u, sel_ut), (sel_d, sel_dt))):
            order_row = sm[s, 1:2, which * LN : (which + 1) * LN].astype(jnp.int32)
            order_flat = jnp.broadcast_to(order_row, (512, LN))
            order_col = jnp.transpose(
                jnp.broadcast_to(sm[s, 1:2, which * LN : (which + 1) * LN], (512, LN))
            ).astype(jnp.int32)
            v0 = iota((512, LN), 0)
            v1 = iota((LN, 512), 1)
            for c in range(4):
                hit_t = (order_flat == (v0 // 16) * 4 + v0 % 4) & ((v0 // 4) % 4 == c)
                sel_t[s, :, c * LN : (c + 1) * LN] = jnp.where(hit_t, 1.0, 0.0).astype(BF)
                hit = (order_col == (v1 // 16) * 4 + v1 % 4) & ((v1 // 4) % 4 == c)
                sel[s, c * LN : (c + 1) * LN, :] = jnp.where(hit, 1.0, 0.0).astype(BF)

    def prepare_mid(s):
        ident = eye[...]
        for c in range(8):
            t_m[s, c] = mm_nt(ident, w_m[s, c]).astype(BF)
            t_l[s, c] = mm_nt(ident, w_l[s, c]).astype(BF)

    def prepare_out(s):
        ident = eye[...]
        for b in range(2):
            t_o[s, b] = mm_nt(ident, w_o[s, b]).astype(BF)

    def send_part(way, s):
        def one(k, carry):
            pltpu.make_async_remote_copy(
                part.at[way, s], parts.at[way, s, me], p_send.at[way, s], p_recv.at[way, s],
                device_id=(seg, peer(k)), device_id_type=MESH,
            ).start()
            return carry

        lax.fori_loop(0, PEERS - 1, one, 0, unroll=PEERS - 1 if way == 1 else 1)
        pltpu.make_async_copy(part.at[way, s], parts.at[way, s, me], p_recv.at[way, s]).start()

    def wait_part(way, s):
        whole = parts.at[way, s]
        pltpu.make_async_copy(whole, whole, p_recv.at[way, s]).wait()
        return jnp.sum(parts[way, s].reshape(PEERS, LN), axis=0, keepdims=True)

    def send_a(way, s):
        for q in range(2):

            def one(k, carry):
                to = peer(k)
                pltpu.make_async_remote_copy(
                    s_a.at[way, s, to, q], r_a.at[way, s, q, me], a_send.at[way, s],
                    a_recv.at[way, s, q], device_id=(seg, to), device_id_type=MESH,
                ).start()
                return carry

            lax.fori_loop(0, PEERS - 1, one, 0, unroll=PEERS - 1 if way == 1 else 1)
            pltpu.make_async_copy(
                s_a.at[way, s, me, q], r_a.at[way, s, q, me], a_recv.at[way, s, q]
            ).start()

    def send_b(way, s, q):
        def one(k, carry):
            to = peer(k)
            pltpu.make_async_remote_copy(
                s_b.at[way, s, q, to], r_b.at[way, s, me, q], b_send.at[way, s],
                b_recv.at[way, s], device_id=(seg, to), device_id_type=MESH,
            ).start()
            return carry

        lax.fori_loop(0, PEERS - 1, one, 0, unroll=PEERS - 1 if way == 1 else 1)
        pltpu.make_async_copy(
            s_b.at[way, s, q, me], r_b.at[way, s, me, q], b_recv.at[way, s]
        ).start()

    def wait_whole(ref, sem):
        pltpu.make_async_copy(ref, ref, sem).wait()

    def shuffle_out(way, s):
        for m in range(4):
            rows = jnp.concatenate([hn[l, m * 64 : (m + 1) * 64, :] for l in range(4)], axis=0)
            out = mm(perm[...], rows).astype(BF)
            s_a[way, s, m * 8 : (m + 1) * 8] = out.reshape(8, 2, 16, LN)

    def shuffle_in(way, s, store):
        for m in range(4):
            rows = r_b[way, s, m * 8 : (m + 1) * 8].reshape(256, LN)
            out = mm(perm_t[...], rows).astype(BF)
            for l in range(4):
                store(l, m, out[l * 64 : (l + 1) * 64])

    def start_back(s):
        e16 = e_c[...].astype(BF)
        for b in range(2):
            dg = mm(w_o[s, b], e16[b * LN : (b + 1) * LN]).astype(BF)
            hn[2 * b] = dg[:256]
            hn[2 * b + 1] = dg[256:]
        shuffle_out(1, s)
        send_a(1, s)

    def gather_g(s):
        wait_whole(r_b.at[0, s], b_recv.at[0, s])

        def store(l, m, value):
            g_n[s, l, m * 64 : (m + 1) * 64, :] = value

        shuffle_in(0, s, store)

    def after_a(s):
        if s == 0:
            second(0, 2)
            third(0, 2)
            for n in (3, 4):
                second(0, n)
                third(0, n)
            send_weights(1)
            send_weights(2)
        final(s, 2)
        final(s, 3)
        prepare_mid(s)

    def after_b(s):
        if s == 0:
            send_weights(3)
        final(s, 4)
        prepare_out(s)
        final_small(s + 1)
        final(s + 1, 1)
        prepare_in(s + 1)

    def forward(s):
        x = xs[s].astype(F32)
        part[0, s] = jnp.sum(x * x, axis=0, keepdims=True)
        send_part(0, s)
        xg[s] = (x * g_t[s]).astype(BF)
        for b in range(2):
            h = mm(t_i[s, b], xg[s, b * LN : (b + 1) * LN]).astype(BF)
            hn[2 * b] = h[:256]
            hn[2 * b + 1] = h[256:]
        shuffle_out(0, s)
        send_a(0, s)
        after_a(s)
        if s == SEC - 1:
            final(s, 4)
            start_back(s)
        r = lax.rsqrt(wait_part(0, s) / D + epsilon)
        r_s[s] = r
        for q in range(2):
            wait_whole(r_a.at[0, s, q], a_recv.at[0, s, q])
            v = mm(sel_u[s], r_a[0, s, q].reshape(512, LN)).astype(BF)
            v_n[s, q * 4 : (q + 1) * 4] = v.reshape(4, LN, LN)
            for c in range(q * 4, q * 4 + 4):
                u = mm(t_m[s, c], v_n[s, c]) * r
                value, slope = gelu_pair(u)
                a = value.astype(BF)
                u_s[s, c] = u
                sl[s, c] = slope
                a_s[s, c] = a
                zq[c] = mm(t_l[s, c], a).astype(BF)
            z = mm(sel_dt[s], zq[q * 4 : (q + 1) * 4].reshape(512, LN)).astype(BF)
            s_b[0, s, q] = z.reshape(PEERS, 16, LN)
            send_b(0, s, q)
        if s < SEC - 1:
            after_b(s)
            gather_g(s)
            for b in range(2):
                y = mm(t_o[s, b], g_n[s, 2 * b : 2 * b + 2].reshape(512, LN))
                xs[s + 1, b * LN : (b + 1) * LN] = (
                    xs[s, b * LN : (b + 1) * LN].astype(F32) + y
                ).astype(BF)

    xs[0] = jnp.transpose(tok[seg].astype(F32)).astype(BF)
    e_c[...] = jnp.transpose(cot[seg].astype(F32))
    second(0, 1)
    third(0, 1)
    final_small(0)
    final(0, 1)
    prepare_in(0)
    for s in range(SEC):
        forward(s)

    grads = (
        (gs_i, gh_i, gr_i), (gs_m, gh_m, gr_m), (gs_l, gh_l, gr_l), (gs_o, gh_o, gr_o)
    )

    def ship_half(s, n, k, h):
        src, _, dst = grads[n]
        pltpu.make_async_remote_copy(
            half(src, s, h), half(dst, k // 2, h), g_send.at[k // 2, n, h],
            g_recv.at[k // 2, n], device_id=row_at(SEC - k), device_id_type=MESH,
        ).start()

    def ship(s, n):
        src, mid, _ = grads[n]

        @pl.when(near(s, 1))
        def _():
            ship_half(s, n, 1, 1)

        @pl.when(near(s, 3))
        def _():
            ship_half(s, n, 3, 0)

        @pl.when(near(s, 2))
        def _():
            for h, k in enumerate((3, 1)):
                pltpu.make_async_remote_copy(
                    half(src, s, h), mid.at[h], h_send.at[n, h], h_recv.at[h, n],
                    device_id=row_at(k), device_id_type=MESH,
                ).start()

    def combine(s, n):
        src, mid, _ = grads[n]
        size = src.shape[1] // 2
        for h, k in enumerate((1, 3)):

            @pl.when(near(s, k))
            def _():
                wait_whole(mid.at[h], h_recv.at[h, n])
                rows = pl.ds(h * size, size)
                src[s, rows] = (src[s, rows].astype(F32) + mid[h].astype(F32)).astype(BF)
                ship_half(s, n, k, h)

    def ship_gain(s):
        @pl.when(seg != s)
        def _():
            slot = lax.rem(seg - s + SEC - 1, SEC)
            pltpu.make_async_remote_copy(
                gs_g.at[s], gr_g.at[slot], gg_send.at[s], gg_recv.at[slot],
                device_id=(s, me), device_id_type=MESH,
            ).start()

    def backward(i, carry):
        s = SEC - 1 - i
        own = seg == s

        def emit(out_ref, send_ref, index, value):
            @pl.when(own)
            def _():
                out_ref[index] = value

            @pl.when(jnp.logical_not(own))
            def _():
                send_ref[(s, *index)] = value.astype(BF)

        e16 = e_c[...].astype(BF)

        @pl.when(i == 0)
        def _():
            gather_g(s)

        for b in range(2):
            emit(
                o_out, gs_o, (b,),
                mm_nt(g_n[s, 2 * b : 2 * b + 2].reshape(512, LN), e16[b * LN : (b + 1) * LN]),
            )
        ship(s, 3)

        @pl.when(i > 0)
        def _():
            combine(s + 1, 2)
            combine(s + 1, 1)

        r = r_s[s]
        sum_u[...] = jnp.zeros_like(sum_u)
        for q in range(2):
            wait_whole(r_a.at[1, s, q], a_recv.at[1, s, q])
            d = mm(sel_d[s], r_a[1, s, q].reshape(512, LN)).astype(BF)
            dz[q * 4 : (q + 1) * 4] = d.reshape(4, LN, LN)
            for c in range(q * 4, q * 4 + 4):
                d_pre = mm(w_l[s, c], dz[c]) * sl[s, c]
                sum_u[...] += jnp.sum(d_pre * u_s[s, c], axis=0, keepdims=True)
                du[c] = (d_pre * r).astype(BF)
            if q == 1:
                part[1, s] = sum_u[...]
                send_part(1, s)
            for c in range(q * 4, q * 4 + 4):
                zq[c] = mm(w_m[s, c], du[c]).astype(BF)
            v = mm(sel_ut[s], zq[q * 4 : (q + 1) * 4].reshape(512, LN)).astype(BF)
            s_b[1, s, q] = v.reshape(PEERS, 16, LN)
            send_b(1, s, q)
        for c in range(8):
            emit(o_low, gs_l, (c,), mm_nt(a_s[s, c], dz[c]))
            emit(o_mid, gs_m, (c,), mm_nt(v_n[s, c], du[c]))
        ship(s, 2)
        ship(s, 1)

        @pl.when(i > 0)
        def _():
            combine(s + 1, 0)

        combine(s, 3)
        total = wait_part(1, s)
        wait_whole(r_b.at[1, s], b_recv.at[1, s])

        def store(l, m, value):
            hn[l, m * 64 : (m + 1) * 64, :] = value

        shuffle_in(1, s, store)
        scale = r * r * total / D
        for b in range(2):
            lo = b * LN
            dh = hn[2 * b : 2 * b + 2].reshape(512, LN)
            emit(o_in, gs_i, (b,), mm_nt(xg[s, lo : lo + LN], dh))
            dn = mm(w_i[s, b], dh)
            x = xs[s, lo : lo + LN].astype(F32)
            gain_grad = jnp.sum(jnp.transpose(dn * x), axis=0, keepdims=True)

            @pl.when(own)
            def _():
                o_gain[:, lo : lo + LN] = gain_grad

            @pl.when(jnp.logical_not(own))
            def _():
                gs_g[s, :, lo : lo + LN] = gain_grad

            e_c[lo : lo + LN] = (
                (e_c[lo : lo + LN] + g_t[s, lo : lo + LN] * dn - x * scale).astype(BF).astype(F32)
            )
        ship(s, 0)
        ship_gain(s)

        @pl.when(s > 0)
        def _():
            start_back(s - 1)

        return carry

    lax.fori_loop(0, SEC, backward, 0)

    combine(0, 2)
    combine(0, 1)
    combine(0, 0)
    outs = (o_in, o_mid, o_low, o_out)
    for n in (3, 2, 1, 0):
        _, _, landed = grads[n]
        for side in range(2):
            wait_whole(landed.at[side], g_recv.at[side, n])
        outs[n][...] += landed[0].astype(F32) + landed[1].astype(F32)
    for slot in range(SEC - 1):
        wait_whole(gr_g.at[slot], gg_recv.at[slot])
    o_gain[...] += gr_g[0] + gr_g[1] + gr_g[2]

    def drain(i, carry):
        way, s = i // SEC, lax.rem(i, SEC)
        wait_whole(parts.at[way, s, pl.ds(0, PEERS - 1)], p_send.at[way, s])
        wait_whole(s_a.at[way, s, pl.ds(0, PEERS - 1)], a_send.at[way, s])
        wait_whole(r_b.at[way, s, pl.ds(0, PEERS - 1)], b_send.at[way, s])
        return carry

    lax.fori_loop(0, 2 * SEC, drain, 0)
    for k in range(SEC - 1):
        wait_whole(small, w_send.at[0, k])
    def passed(*slots):
        for n in range(1, 5):
            for slot in slots:
                wait_whole(half(shared[n][1], 0, slot % 2), w_pass.at[n, slot])

    @pl.when(seg == 0)
    def _():
        for n in range(1, 5):
            for h in range(2):
                wait_whole(half(shared[n][1], 0, h), w_send.at[n, h])

    @pl.when(seg > 0)
    def _():
        for n in range(1, 5):
            for k in range(SEC - 1):
                wait_whole(shared[n][0], w_send.at[n, k])

    @pl.when(seg == 1)
    def _():
        passed(0)

    @pl.when(seg == 2)
    def _():
        passed(2, 3)

    @pl.when(seg == 3)
    def _():
        passed(1)

    for n, (_, mid, landed) in enumerate(grads):
        for h in range(2):
            wait_whole(mid.at[h], h_send.at[n, h])
            for side in range(2):
                wait_whole(half(landed, side, h), g_send.at[side, n, h])

    def drain_gain(s, carry):
        @pl.when(seg != s)
        def _():
            wait_whole(gs_g.at[s], gg_send.at[s])

        return carry

    lax.fori_loop(0, SEC, drain_gain, 0)


def shards(tokens, cotangent, gain, weight_in, weight_mid, weight_low, weight_out, up, down):
    order = jnp.concatenate([up, down], axis=1).astype(F32)
    small = jnp.concatenate([gain, order, jnp.zeros((6, 256), F32)], axis=0)
    vm = pltpu.VMEM
    dma = pltpu.SemaphoreType.DMA
    scratch = [
        vm((SEC, 2, LN, 512), BF), vm((SEC, 8, LN, LN), BF), vm((SEC, 8, LN, LN), BF),
        vm((SEC, 2, 512, LN), BF), vm((SEC, 8, 256), F32),
        vm((SEC, 2, 512, LN), BF), vm((SEC, 8, LN, LN), BF), vm((SEC, 8, LN, LN), BF),
        vm((SEC, 2, LN, 512), BF),
        vm((SEC, 512, 512), BF), vm((SEC, 512, 512), BF), vm((SEC, 512, 512), BF),
        vm((SEC, 512, 512), BF), vm((SEC, 256, LN), F32),
        vm((256, 256), BF), vm((256, 256), BF), vm((LN, LN), BF),
        vm((SEC, 256, LN), BF), vm((SEC, 256, LN), BF), vm((2, SEC, 1, LN), F32),
        vm((2, SEC, PEERS, 1, LN), F32), vm((SEC, 1, LN), F32), vm((4, 256, LN), BF),
        vm((2, SEC, PEERS, 2, 16, LN), BF), vm((2, SEC, 2, PEERS, 16, LN), BF),
        vm((2, SEC, 2, PEERS, 16, LN), BF), vm((2, SEC, PEERS, 2, 16, LN), BF),
        vm((SEC, 8, LN, LN), BF), vm((SEC, 8, LN, LN), F32), vm((SEC, 8, LN, LN), F32),
        vm((SEC, 8, LN, LN), BF), vm((SEC, 4, 256, LN), BF),
        vm((8, LN, LN), BF), vm((8, LN, LN), BF), vm((8, LN, LN), BF),
        vm((256, LN), F32), vm((1, LN), F32),
        vm((SEC, 2, LN, 512), BF), vm((SEC, 8, LN, LN), BF), vm((SEC, 8, LN, LN), BF),
        vm((SEC, 2, 512, LN), BF), vm((SEC, 1, 256), F32),
        vm((2, 1, LN, 512), BF), vm((2, 4, LN, LN), BF), vm((2, 4, LN, LN), BF),
        vm((2, 1, 512, LN), BF),
        vm((2, 2, LN, 512), BF), vm((2, 8, LN, LN), BF), vm((2, 8, LN, LN), BF),
        vm((2, 2, 512, LN), BF), vm((3, 1, 256), F32),
        dma((5, SEC - 1)), dma((SEC, 5, 2)), dma((5, 4)),
        dma((2, SEC)), dma((2, SEC)), dma((2, SEC)),
        dma((2, SEC, 2)), dma((2, SEC)), dma((2, SEC)),
        dma((2, 4, 2)), dma((2, 4)), dma((4, 2)), dma((2, 4)), dma((SEC,)), dma((3,)),
    ]
    whole = pl.BlockSpec(memory_space=pltpu.VMEM)
    g_in, g_mid, g_low, g_out, g_gain = pl.pallas_call(
        kernel,
        out_shape=[
            jax.ShapeDtypeStruct((2, LN, 512), F32),
            jax.ShapeDtypeStruct((8, LN, LN), F32),
            jax.ShapeDtypeStruct((8, LN, LN), F32),
            jax.ShapeDtypeStruct((2, 512, LN), F32),
            jax.ShapeDtypeStruct((1, 256), F32),
        ],
        in_specs=[whole] * 7,
        out_specs=[whole] * 5,
        scratch_shapes=scratch,
        compiler_params=pltpu.CompilerParams(
            collective_id=0, has_side_effects=True, vmem_limit_bytes=60 << 20
        ),
    )(tokens, cotangent, small, weight_in[0], weight_mid[0], weight_low[0], weight_out[0])
    return g_in[None], g_mid[None], g_low[None], g_out[None], g_gain


def solution(mesh):
    in_specs = (
        P(None, None, "hid"),
        P(None, None, "hid"),
        P("segment", "hid"),
        P("segment", "hid", None, None),
        P("segment", "hid", None, None),
        P("segment", "hid", None, None),
        P("segment", "hid", None, None),
        P("segment", None),
        P("segment", None),
    )
    out_specs = (
        P("segment", "hid", None, None),
        P("segment", "hid", None, None),
        P("segment", "hid", None, None),
        P("segment", "hid", None, None),
        P("segment", "hid"),
    )
    return jax.shard_map(shards, mesh=mesh, in_specs=in_specs, out_specs=out_specs, check_vma=False)
```
